256 devices in a mesh: grp: 4 (over y), blk: 64 (over z, x, core).
Axes of the slice: x: 4, y: 4, z: 8, core: 2. Of those that a mesh axis runs over, the one named last changes fastest.
Arguments:
- rhs: bfloat16 [1, 768, 4096], P(None, 'blk', 'grp'), may hold values from -6 to 6
- lower_factor_tiles: bfloat16 [1, 32768, 1024], P(None, ('grp', 'blk')), may hold values from -0.09375 to 0.09375
- tile_rows: int32 [1, 4, 128], P(None, 'grp'), may hold values from 16 to 192, as said below
- diag_inv: bfloat16 [1, 4096, 512], P(None, 'grp'), as said below
- inner_block: bfloat16 [1, 2048, 512], P(None, 'grp'), may hold values from -0.1875 to 0.1875
- lower_row_solution: bfloat16 [768, 8192], P('blk'), may hold values from -6 to 6
Outputs:
- forward_solution: bfloat16 [1, 768, 4096], P(None, 'blk', 'grp')
- pending_lower_updates: float32 [768, 8192], P('blk', 'grp')
- solution: bfloat16 [1, 768, 4096], P(None, 'blk', 'grp')
The draws below stay inside these ranges and needn't reach their ends.
Inputs may be any that keep to these rules, and one draw needn't show every extreme that they name: tile_rows[r, g] gives for each of the 128 slots of panel p = r * 4 + g a row tile below that panel, at least (p + 1) * 16, or 192 for an empty slot; no row tile appears twice in one panel. `diag_inv`: each 512 x 512 block is upper triangular.
All inputs are finite; a program needn't handle non-finite values.
Results may differ from the reference program's by a relative error of at most 0.0085.
Values may be sent and summed in bfloat16 or wider, within the bound.
No kernel may reach another device: no remote copies, remote signals or barrier semaphores. Data moves between devices by JAX's collectives and lax.ppermute only.
A program may use at most 64 MiB of HBM per device.

```python
import math
import jax
import jax.numpy as jnp
from jax import lax

S = 512
KB = 2
TILE_HEIGHT = 64
GROUP_PANELS = 1
LOAD_CASES = 768
PANEL_COLUMNS = 1024
SLOT_TOTAL = 128
ROW_TILES = 192
N_GRP = 4


def shuffled(subkey):
    return jax.random.permutation(subkey, ROW_TILES)


def draw_tile_rows(key, part):
    key = jax.random.fold_in(key, 11)
    order_key, retain_sort_key = jax.random.split(key)
    total_panel_count = GROUP_PANELS * N_GRP
    sort_orders = jax.vmap(shuffled)(jax.random.split(order_key, total_panel_count)).astype(jnp.int32)
    first_below = (jnp.arange(total_panel_count, dtype=jnp.int32)[:, None] + 1) * (PANEL_COLUMNS // TILE_HEIGHT)
    room = ROW_TILES - first_below
    outside = (sort_orders >= room).astype(jnp.int32)
    ranked_tiles = jnp.argsort(outside, axis=1, stable=True)
    selected_tiles = jnp.take_along_axis(sort_orders, ranked_tiles[:, :SLOT_TOTAL], axis=1)
    selected_rows = (first_below + selected_tiles).astype(jnp.int32)
    retained_tiles = jax.random.randint(retain_sort_key, (total_panel_count, SLOT_TOTAL), 0, 8)
    nearby = selected_rows < first_below + PANEL_COLUMNS // TILE_HEIGHT
    active_flag = nearby | (retained_tiles != 0)
    slot_position = jnp.arange(SLOT_TOTAL, dtype=jnp.int32)[None, :]
    starting_panel = jnp.arange(total_panel_count, dtype=jnp.int32)[:, None] == 0
    active_flag = active_flag & jnp.logical_not(starting_panel & (slot_position == SLOT_TOTAL - 1))
    return jnp.where(active_flag, selected_rows, ROW_TILES).astype(jnp.int32).reshape(GROUP_PANELS, N_GRP, SLOT_TOTAL)


def draw_diag_inv(key, part):
    key = jax.random.fold_in(key, 23)
    full_shape = (GROUP_PANELS, N_GRP * KB * S, S)
    row_pos = lax.broadcasted_iota(jnp.int32, full_shape, 1) % S
    col_pos = lax.broadcasted_iota(jnp.int32, full_shape, 2)
    above_diag = (col_pos > row_pos).astype(jnp.float32)
    diagonal = (col_pos == row_pos).astype(jnp.float32)
    spread = jax.random.normal(key, full_shape, jnp.float32) * (0.8 / math.sqrt(S))
    return (0.8 * diagonal + spread * above_diag).astype(jnp.bfloat16)


def levels(own_key, extent, cuts, low, high):
    gain, own = 1.0, jax.random.fold_in(own_key, 6)
    for dim, shards_of in cuts:
        heights = jnp.exp(jax.random.uniform(jax.random.fold_in(own, dim), (shards_of,), jnp.float32, low / len(cuts), high / len(cuts)))
        gain = gain * jnp.repeat(heights, extent[dim] // shards_of).reshape([-1 if axis == dim else 1 for axis in range(len(extent))])
    return gain


def centred(own_key, shape, deviation, limit, cuts=(), held_as=jnp.bfloat16):
    gain = levels(own_key, shape, cuts, -0.22, 0.18) if cuts else 1.0
    array = jax.random.normal(own_key, shape, jnp.float32) * deviation * gain
    return jnp.minimum(jnp.maximum(array, -limit), limit).astype(held_as)


def setup_inputs(seed: int = 0) -> dict:
    key_list = jax.random.split(jax.random.key(seed), 7)
    return {
        "rhs": centred(key_list[0], (GROUP_PANELS, LOAD_CASES, N_GRP * PANEL_COLUMNS), 1.0, 6.0, ((1, 64), (2, 4))),
        "lower_factor_tiles": centred(key_list[1], (GROUP_PANELS, N_GRP * SLOT_TOTAL * TILE_HEIGHT, PANEL_COLUMNS), (4 * PANEL_COLUMNS) ** -0.5, 0.09375, ((1, 256),)),
        "tile_rows": draw_tile_rows(jax.random.fold_in(key_list[6], 71), 0),
        "diag_inv": draw_diag_inv(jax.random.fold_in(key_list[6], 71), 0),
        "inner_block": centred(key_list[4], (GROUP_PANELS, N_GRP * S, S), (2 * S) ** -0.5, 0.1875, ((1, 4),)),
        "lower_row_solution": centred(key_list[5], (LOAD_CASES, SLOT_TOTAL * TILE_HEIGHT), 1.0, 6.0, ((0, 64),)),
    }


def lower_solve(residue, inverse, coupling):
    highest = lax.Precision.HIGHEST
    split_at = inverse.shape[1]
    leading = jnp.dot(residue[:, :split_at], inverse[:split_at].astype(jnp.float32), precision=highest).astype(jnp.bfloat16)
    leading_kept = lax.optimization_barrier(leading)
    carried = residue[:, split_at:] - jnp.dot(leading_kept.astype(jnp.float32), coupling.astype(jnp.float32), precision=highest)
    second = jnp.dot(carried, inverse[split_at:].astype(jnp.float32), precision=highest).astype(jnp.bfloat16)
    return jnp.concatenate([leading, second], axis=1)


def upper_solve(residue, inverse, coupling):
    highest = lax.Precision.HIGHEST
    split_at = inverse.shape[1]
    contract = (((1,), (1,)), ((), ()))
    second = lax.dot_general(residue[:, split_at:], inverse[split_at:].astype(jnp.float32), contract, precision=highest).astype(jnp.bfloat16)
    second_kept = lax.optimization_barrier(second)
    carried = residue[:, :split_at] - lax.dot_general(second_kept.astype(jnp.float32), coupling.astype(jnp.float32), contract, precision=highest)
    leading = lax.dot_general(carried, inverse[:split_at].astype(jnp.float32), contract, precision=highest).astype(jnp.bfloat16)
    return jnp.concatenate([leading, second], axis=1)


def assemble(pieces):
    load_case_count = pieces[0].shape[0]
    stacked = jnp.stack(pieces).reshape(GROUP_PANELS, N_GRP, load_case_count, PANEL_COLUMNS)
    return jnp.transpose(stacked, (0, 2, 1, 3)).reshape(GROUP_PANELS, load_case_count, N_GRP * PANEL_COLUMNS)


def reference(rhs, lower_factor_tiles, tile_rows, diag_inv, inner_block, lower_row_solution):
    load_case_count = rhs.shape[1]
    total_panel_count = GROUP_PANELS * N_GRP
    tiles_per_panel = PANEL_COLUMNS // TILE_HEIGHT
    visible_tiles = total_panel_count * tiles_per_panel
    outstanding_updates = jnp.zeros((load_case_count, ROW_TILES + 1, TILE_HEIGHT), jnp.float32)
    forward_parts = []
    for panel_index in range(total_panel_count):
        panel_round_index = panel_index // N_GRP
        group_member = panel_index % N_GRP
        given_rhs = rhs[panel_round_index, :, group_member * PANEL_COLUMNS:(group_member + 1) * PANEL_COLUMNS].astype(jnp.float32)
        owed_rows = outstanding_updates[:, panel_index * tiles_per_panel:(panel_index + 1) * tiles_per_panel, :].reshape(load_case_count, PANEL_COLUMNS)
        inverse = diag_inv[panel_round_index, group_member * KB * S:(group_member + 1) * KB * S]
        coupling = inner_block[panel_round_index, group_member * S:(group_member + 1) * S]
        tile_collection = lower_factor_tiles[panel_round_index, group_member * SLOT_TOTAL * TILE_HEIGHT:(group_member + 1) * SLOT_TOTAL * TILE_HEIGHT]
        row_numbers = tile_rows[panel_round_index, group_member]
        solved = lower_solve(given_rhs - owed_rows, inverse, coupling)
        forward_parts.append(solved)
        row_update = lax.dot_general(solved, tile_collection, (((1,), (1,)), ((), ())), preferred_element_type=jnp.float32)
        outstanding_updates = outstanding_updates.at[:, row_numbers, :].add(row_update.reshape(load_case_count, SLOT_TOTAL, TILE_HEIGHT))
    pending_lower_updates = outstanding_updates[:, visible_tiles:ROW_TILES, :].reshape(load_case_count, SLOT_TOTAL * TILE_HEIGHT)
    finished_rows = jnp.zeros((load_case_count, ROW_TILES + 1, TILE_HEIGHT), jnp.bfloat16)
    finished_rows = finished_rows.at[:, visible_tiles:ROW_TILES, :].set(lower_row_solution.reshape(load_case_count, SLOT_TOTAL, TILE_HEIGHT))
    backward_parts = [None] * total_panel_count
    for panel_index in reversed(range(total_panel_count)):
        panel_round_index = panel_index // N_GRP
        group_member = panel_index % N_GRP
        inverse = diag_inv[panel_round_index, group_member * KB * S:(group_member + 1) * KB * S]
        coupling = inner_block[panel_round_index, group_member * S:(group_member + 1) * S]
        tile_collection = lower_factor_tiles[panel_round_index, group_member * SLOT_TOTAL * TILE_HEIGHT:(group_member + 1) * SLOT_TOTAL * TILE_HEIGHT]
        row_numbers = tile_rows[panel_round_index, group_member]
        collected_rows = finished_rows[:, row_numbers, :].reshape(load_case_count, SLOT_TOTAL * TILE_HEIGHT)
        transposed = jnp.dot(collected_rows, tile_collection, preferred_element_type=jnp.float32)
        solved = upper_solve(forward_parts[panel_index].astype(jnp.float32) - transposed, inverse, coupling)
        backward_parts[panel_index] = solved
        finished_rows = finished_rows.at[:, panel_index * tiles_per_panel:(panel_index + 1) * tiles_per_panel, :].set(solved.reshape(load_case_count, tiles_per_panel, TILE_HEIGHT))
    return assemble(forward_parts), pending_lower_updates, assemble(backward_parts)
```

```python
import functools

import jax
import jax.numpy as jnp
from jax import lax
from jax.experimental import pallas as pl
from jax.experimental.pallas import tpu as pltpu
from jax.sharding import PartitionSpec as P

TILE = 64
ROWS = 16
CHUNK = 16
GROUPS = 4
BF = jnp.bfloat16
F32 = jnp.float32
VMEM_LIMIT = 48 * 1024 * 1024
NT = (((1,), (1,)), ((), ()))


def mm(a, b):
    return jnp.dot(a, b, preferred_element_type=F32)


def mm_nt(a, b):
    return lax.dot_general(a, b, NT, preferred_element_type=F32)


def split_mm(product, r, w):
    high = r.astype(BF)
    low = (r - high.astype(F32)).astype(BF)
    both = product(jnp.concatenate([high, low], axis=0), w)
    return both[: r.shape[0]] + both[r.shape[0] :]


def lower_solve(residue, inverse, coupling):
    half = coupling.shape[0]
    leading = split_mm(mm, residue[:, :half], inverse[:half]).astype(BF)
    carried = residue[:, half:] - mm(leading, coupling[...])
    second = split_mm(mm, carried, inverse[half:]).astype(BF)
    return leading, second


def upper_solve(residue, inverse, coupling):
    half = coupling.shape[0]
    second = split_mm(mm_nt, residue[:, half:], inverse[half:]).astype(BF)
    carried = residue[:, :half] - mm_nt(second, coupling[...])
    leading = split_mm(mm_nt, carried, inverse[:half]).astype(BF)
    return leading, second


def fetch_tiles(slots, factor, tiles, sems):
    copies = []
    for i in range(CHUNK):
        start = pl.multiple_of(slots[i] * TILE, TILE)
        copy = pltpu.make_async_copy(
            factor.at[pl.ds(start, TILE)], tiles.at[pl.ds(i * TILE, TILE)], sems.at[i]
        )
        copy.start()
        copies.append(copy)
    return copies


def forward_kernel(received_count, slots, factor, mask, acc, inverse, coupling, *rest):
    received = rest[:received_count]
    acc_out, solved_out, message_out, tiles, sems = rest[received_count:]
    copies = fetch_tiles(slots, factor, tiles, sems)
    residue = acc[...]
    for ref in received:
        residue = residue - ref[...].astype(F32)
    acc_out[...] = residue
    half = coupling.shape[0]
    leading, second = lower_solve(residue, inverse, coupling)
    solved_out[:, :half] = leading
    solved_out[:, half:] = second
    for copy in copies:
        copy.wait()
    product = mm_nt(solved_out[...], tiles[...])
    message_out[...] = (product * mask[...]).astype(BF)


def backward_kernel(received_count, slots, factor, mask, acc, inverse, coupling, *rest):
    received = rest[:received_count]
    acc_out, solved_out = rest[received_count : received_count + 2]
    residue = acc[...]
    if received:
        tiles, sems = rest[received_count + 2 :]
        copies = fetch_tiles(slots, factor, tiles, sems)
        for ref in received[1:]:
            residue = residue - ref[...]
        masked = received[0][...] * mask[...].astype(BF)
        for copy in copies:
            copy.wait()
        residue = residue - mm(masked, tiles[...])
    acc_out[...] = residue
    half = coupling.shape[0]
    leading, second = upper_solve(residue, inverse, coupling)
    solved_out[:, :half] = leading
    solved_out[:, half:] = second


def whole(x):
    return pl.BlockSpec(x.shape, lambda i, *_: (0,) * len(x.shape))


def chain_call(kernel, slots, factor, mask, acc, inverse, coupling, received, out_shapes, with_tiles):
    width = acc.shape[1]
    operands = [mask, acc, inverse, coupling, *received]
    scratch = []
    if with_tiles:
        scratch = [
            pltpu.VMEM((CHUNK * TILE, width), BF),
            pltpu.SemaphoreType.DMA((CHUNK,)),
        ]
    return pl.pallas_call(
        functools.partial(kernel, len(received)),
        grid_spec=pltpu.PrefetchScalarGridSpec(
            num_scalar_prefetch=1,
            grid=(1,),
            in_specs=[pl.BlockSpec(memory_space=pl.ANY)] + [whole(x) for x in operands],
            out_specs=[whole(x) for x in out_shapes],
            scratch_shapes=scratch,
        ),
        out_shape=out_shapes,
        compiler_params=pltpu.CompilerParams(vmem_limit_bytes=VMEM_LIMIT),
        cost_estimate=pl.CostEstimate(
            flops=4 * ROWS * width * width, bytes_accessed=8 * width * width, transcendentals=0
        ),
    )(slots, factor, *operands)


def tile_specs(width):
    def spec(j):
        return pl.BlockSpec((TILE, width), lambda i, slots: (slots[i * CHUNK + j], 0))

    return [spec(j) for j in range(CHUNK)]


def spread_kernel(slots, solved, mask, *rest):
    tiles, out = rest[:CHUNK], rest[CHUNK]
    stacked = jnp.concatenate([t[...] for t in tiles], axis=0)
    out[...] = (mm_nt(solved[...], stacked) * mask[...]).astype(out.dtype)


def spread(slots, solved, mask, factor):
    width = solved.shape[1]
    count = slots.shape[0] // CHUNK
    return pl.pallas_call(
        spread_kernel,
        grid_spec=pltpu.PrefetchScalarGridSpec(
            num_scalar_prefetch=1,
            grid=(count,),
            in_specs=[
                pl.BlockSpec((ROWS, width), lambda i, slots: (0, 0)),
                pl.BlockSpec((1, CHUNK * TILE), lambda i, slots: (0, i)),
            ]
            + tile_specs(width),
            out_specs=pl.BlockSpec((ROWS, CHUNK * TILE), lambda i, slots: (0, i)),
        ),
        out_shape=jax.ShapeDtypeStruct((ROWS, count * CHUNK * TILE), BF),
        compiler_params=pltpu.CompilerParams(vmem_limit_bytes=VMEM_LIMIT),
        cost_estimate=pl.CostEstimate(
            flops=2 * ROWS * width * width * count,
            bytes_accessed=2 * width * width * count,
            transcendentals=0,
        ),
    )(slots, solved, mask, *([factor] * CHUNK))


def collect_kernel(slots, rows, mask, *rest):
    tiles, out = rest[:CHUNK], rest[CHUNK]

    @pl.when(pl.program_id(0) == 0)
    def _():
        out[...] = jnp.zeros_like(out)

    stacked = jnp.concatenate([t[...] for t in tiles], axis=0)
    out[...] += mm(rows[...] * mask[...].astype(BF), stacked)


def collect(slots, rows, mask, factor):
    width = factor.shape[1]
    count = slots.shape[0] // CHUNK
    return pl.pallas_call(
        collect_kernel,
        grid_spec=pltpu.PrefetchScalarGridSpec(
            num_scalar_prefetch=1,
            grid=(count,),
            in_specs=[
                pl.BlockSpec((ROWS, CHUNK * TILE), lambda i, slots: (0, i)),
                pl.BlockSpec((1, CHUNK * TILE), lambda i, slots: (0, i)),
            ]
            + tile_specs(width),
            out_specs=pl.BlockSpec((ROWS, width), lambda i, slots: (0, 0)),
        ),
        out_shape=jax.ShapeDtypeStruct((ROWS, width), F32),
        compiler_params=pltpu.CompilerParams(vmem_limit_bytes=VMEM_LIMIT),
        cost_estimate=pl.CostEstimate(
            flops=2 * ROWS * width * width * count,
            bytes_accessed=2 * width * width * count,
            transcendentals=0,
        ),
    )(slots, rows, mask, *([factor] * CHUNK))


def body(rhs, lower_factor_tiles, tile_rows, diag_inv, inner_block, lower_row_solution):
    _, cases, width = rhs.shape
    group = lax.axis_index("grp")
    table = tile_rows[0, 0]
    slot_count = table.shape[0]
    inverse, coupling = diag_inv[0], inner_block[0]
    per_panel = width // TILE
    chain_tiles = GROUPS * per_panel
    lower_tiles = lower_row_solution.shape[1] // TILE
    tile_count = chain_tiles + lower_tiles

    def grow(x):
        return jnp.pad(x, ((0, ROWS - cases), (0, 0)))

    def send(x, pairs):
        return lax.ppermute(x, "grp", pairs)

    here = table[None, :] == jnp.arange(tile_count, dtype=jnp.int32)[:, None]
    slot_of = jnp.sum(
        jnp.where(here, jnp.arange(slot_count, dtype=jnp.int32)[None, :], 0), axis=1
    )
    present = jnp.any(here, axis=1)
    numbers = jnp.arange(tile_count, dtype=jnp.int32)
    first = (group + 1) * per_panel
    near_slots = lax.dynamic_slice_in_dim(slot_of, first, 3 * per_panel)
    near_mask = lax.dynamic_slice_in_dim(present & (numbers < chain_tiles), first, 3 * per_panel)
    quarter = lower_tiles // GROUPS
    turned = lambda x: jnp.roll(x.reshape(GROUPS, quarter), -group, axis=0).reshape(-1)
    wide = lambda m: jnp.repeat(m.astype(F32), TILE)[None, :]
    low_slots, low_present = slot_of[chain_tiles:], present[chain_tiles:]
    low_mask = wide(low_present)
    turned_slots, turned_mask = turned(low_slots), wide(turned(low_present))
    near_mask = wide(near_mask)
    panel = per_panel * TILE
    slots1, mask1 = near_slots[:per_panel], near_mask[:, :panel]
    slots23, mask23 = near_slots[per_panel:], near_mask[:, panel:]

    factor = lax.all_gather(lower_factor_tiles[0], "blk", axis=0, tiled=True)

    rows_shape = lambda dtype: jax.ShapeDtypeStruct((ROWS, width), dtype)
    owed_low = collect(low_slots, grow(lower_row_solution), low_mask, factor)

    acc = grow(rhs[0]).astype(F32)
    received, later = [], {}
    for step in range(GROUPS):
        acc, solved, message = chain_call(
            forward_kernel, slots1, factor, mask1, acc, inverse, coupling, received,
            [rows_shape(F32), rows_shape(BF), rows_shape(BF)], True,
        )
        if step == GROUPS - 1:
            break
        received = [send(message, [(step, step + 1)])]
        if step + 2 < GROUPS:
            far = spread(slots23, solved, mask23, factor)
            for hop in range(2, GROUPS - step):
                part = far[:, (hop - 2) * panel : (hop - 1) * panel]
                later.setdefault(step + 2, []).append(send(part, [(step, step + hop)]))
        received += later.pop(step + 1, [])

    beyond = spread(turned_slots, solved, turned_mask, factor)[:cases]
    part = lower_tiles * TILE // GROUPS
    pending = beyond[:, :part].astype(F32)
    for hop in range(1, GROUPS):
        pending = pending + send(
            beyond[:, hop * part : (hop + 1) * part],
            [(g, (g + hop) % GROUPS) for g in range(GROUPS)],
        ).astype(F32)

    acc = solved.astype(F32) - owed_low
    received = []
    for step in range(GROUPS):
        acc, settled = chain_call(
            backward_kernel, slots1, factor, mask1, acc, inverse, coupling, received,
            [rows_shape(F32), rows_shape(BF)], bool(received),
        )
        if step == GROUPS - 1:
            break
        holder = GROUPS - 1 - step
        received = [send(settled, [(holder, holder - 1)])]
        if holder >= 2:
            far = [send(settled, [(holder, holder - hop)]) for hop in range(2, holder + 1)]
            while len(far) < 2:
                far.append(jnp.zeros_like(settled))
            later.setdefault(step + 2, []).append(
                collect(slots23, jnp.concatenate(far, axis=1), mask23, factor)
            )
        received += later.pop(step + 1, [])

    return (solved[None, :cases], pending, settled[None, :cases])


def solution(mesh):
    placed = (
        P(None, "blk", "grp"),
        P(None, ("grp", "blk"), None),
        P(None, "grp", None),
        P(None, "grp", None),
        P(None, "grp", None),
        P("blk", None),
    )
    return jax.shard_map(
        body,
        mesh=mesh,
        in_specs=placed,
        out_specs=(P(None, "blk", "grp"), P("blk", "grp"), P(None, "blk", "grp")),
        check_vma=False,
    )
```

```python
import functools

import jax
import jax.numpy as jnp
from jax import lax
from jax.experimental import pallas as pl
from jax.experimental.pallas import tpu as pltpu
from jax.sharding import PartitionSpec as P

TILE = 64
GROUPS = 4
ROWS = 16
BLOCK, DEPTH = 512, 6
BF = jnp.bfloat16
F32 = jnp.float32
VMEM_LIMIT = 20 * 1024 * 1024
NT = (((1,), (1,)), ((), ()))


def mm(a, b):
    return jnp.dot(a, b, preferred_element_type=F32)


def mm_nt(a, b):
    return lax.dot_general(a, b, NT, preferred_element_type=F32)


def split_mm(product, r, w):
    high = r.astype(BF).astype(F32)
    both = product(jnp.concatenate([high, r - high], axis=0).astype(BF), w)
    return both[: r.shape[0]] + both[r.shape[0] :]


def lower_solve(residue, inverse, coupling):
    half = coupling.shape[0]
    leading = split_mm(mm, residue[:, :half], inverse[:half]).astype(BF)
    carried = residue[:, half:] - mm(leading, coupling[...])
    second = split_mm(mm, carried, inverse[half:]).astype(BF)
    return leading, second


def upper_solve(residue, inverse, coupling):
    half = coupling.shape[0]
    second = split_mm(mm_nt, residue[:, half:], inverse[half:]).astype(BF)
    carried = residue[:, :half] - mm_nt(second, coupling[...])
    return split_mm(mm_nt, carried, inverse[:half]).astype(BF), second


def store_halves(out, leading, second):
    half = leading.shape[1]
    out[:, :half] = leading.astype(out.dtype)
    out[:, half : 2 * half] = second.astype(out.dtype)


def first_kernel(acc, inverse, coupling, solved_out):
    store_halves(solved_out, *lower_solve(acc[...], inverse, coupling))


def build_kernel(places, count, targets, missing, *rest):
    pieces, solved = rest[:count], rest[count]
    near_out, message_out, tiles, sems, out_sems = rest[count + 1 :]
    width = tiles.shape[1]

    def copy(slot):
        piece, start = places[slot]
        to = pl.multiple_of(jnp.maximum(targets[slot], 0) * TILE, TILE)
        return pltpu.make_async_copy(
            pieces[piece].at[pl.ds(start, TILE)], tiles.at[pl.ds(to, TILE)], sems.at[slot]
        )

    for slot in range(len(places)):

        @pl.when(targets[slot] >= 0)
        def _(slot=slot):
            copy(slot).start()

    for i in range(tiles.shape[0] // TILE):

        @pl.when(missing[i] > 0)
        def _(i=i):
            tiles[i * TILE : (i + 1) * TILE, :] = jnp.zeros((TILE, width), BF)

    for slot in range(len(places)):

        @pl.when(targets[slot] >= 0)
        def _(slot=slot):
            copy(slot).wait()

    kept = []
    for n in range(tiles.shape[0] // width):
        part = pl.ds(n * width, width)
        kept.append(pltpu.make_async_copy(tiles.at[part], near_out.at[part], out_sems.at[n]))
        kept[-1].start()
    for n in range(tiles.shape[0] // width):
        part = slice(n * width, (n + 1) * width)
        message_out[:, part] = mm_nt(solved[...], tiles[part, :]).astype(BF)
    for copy_out in kept:
        copy_out.wait()


def in_hbm(x):
    return pltpu.with_memory_space_constraint(x, pltpu.HBM)


def build(pieces, places, targets, missing, solved):
    width = solved.shape[1]
    near_rows = missing.shape[0] * TILE
    anywhere = pl.BlockSpec(memory_space=pl.ANY)
    held = pl.BlockSpec(memory_space=pltpu.HBM)
    return pl.pallas_call(
        functools.partial(build_kernel, places, len(pieces)),
        grid_spec=pltpu.PrefetchScalarGridSpec(
            num_scalar_prefetch=2,
            grid=(1,),
            in_specs=[held] * len(pieces) + [whole(solved)],
            out_specs=[anywhere, pl.BlockSpec((ROWS, near_rows), lambda i, *_: (0, 0))],
            scratch_shapes=[
                pltpu.VMEM((near_rows, width), BF),
                pltpu.SemaphoreType.DMA((len(places),)),
                pltpu.SemaphoreType.DMA((near_rows // width,)),
            ],
        ),
        out_shape=[
            pltpu.VMEM((near_rows, width), BF),
            jax.ShapeDtypeStruct((ROWS, near_rows), BF),
        ],
        compiler_params=pltpu.CompilerParams(vmem_limit_bytes=VMEM_LIMIT),
        cost_estimate=pl.CostEstimate(
            flops=300 * width * width, bytes_accessed=15 * width * width, transcendentals=0
        ),
    )(targets, missing, *map(in_hbm, pieces), solved)


def forward_kernel(near, acc, inverse, coupling, received, acc_out, solved_out, message_out):
    width = acc.shape[1]
    residue = acc[...] - received[:, :width].astype(F32)
    acc_out[...] = residue
    store_halves(solved_out, *lower_solve(residue, inverse, coupling))
    product = mm_nt(solved_out[...], near[...])
    message_out[...] = (product + received[:, width:].astype(F32)).astype(BF)


def turn_kernel(acc, owed, inverse, coupling, received, solved_out, residue_out, message_out):
    residue = acc[...] - received[...].astype(F32)
    store_halves(solved_out, *lower_solve(residue, inverse, coupling))
    residue = solved_out[...].astype(F32) - owed[...]
    residue_out[...] = residue
    store_halves(message_out, *upper_solve(residue, inverse, coupling))


def backward_kernel(near, acc, inverse, coupling, received, acc_out, message_out):
    width = acc.shape[1]
    residue = acc[...] - mm(received[...], near[...])
    acc_out[...] = residue
    store_halves(message_out, *upper_solve(residue, inverse, coupling))
    if message_out.shape[1] > width:
        message_out[:, width:] = received[...]


def whole(x):
    return pl.BlockSpec(x.shape, lambda i, *_: (0,) * len(x.shape))


def step_call(kernel, near, chunks, operands, out_shapes):
    width = out_shapes[0].shape[1]
    specs, first = [], []
    if chunks:
        specs = [pl.BlockSpec((chunks * width, width), lambda i: (0, 0))]
        first = [pltpu.with_memory_space_constraint(near, pltpu.VMEM)]
    return pl.pallas_call(
        kernel,
        grid=(1,),
        in_specs=specs + [whole(x) for x in operands],
        out_specs=[whole(x) for x in out_shapes],
        out_shape=out_shapes,
        compiler_params=pltpu.CompilerParams(vmem_limit_bytes=VMEM_LIMIT),
        cost_estimate=pl.CostEstimate(
            flops=100 * width * width, bytes_accessed=5 * width * width, transcendentals=0
        ),
    )(*first, *operands)


def stream_kernel(blocks, count, spreading, started, rows, *rest):
    pieces, start = rest[:count], rest[count] if started else None
    out, held, sems = rest[count + started :]
    depth, height = held.shape[0], held.shape[1]

    def copy(n):
        piece, first = blocks[n]
        return pltpu.make_async_copy(
            pieces[piece].at[pl.ds(first, height)], held.at[n % depth], sems.at[n % depth]
        )

    for n in range(min(depth, len(blocks))):
        copy(n).start()
    total = start[...] if started else None
    for n in range(len(blocks)):
        copy(n).wait()
        here = slice(n * height, (n + 1) * height)
        if spreading:
            out[:, here] = mm_nt(rows[...], held[n % depth]).astype(out.dtype)
        else:
            product = mm(rows[:, here], held[n % depth])
            total = product if total is None else total + product
        if n + depth < len(blocks):
            copy(n + depth).start()
    if not spreading:
        out[...] = total


def stream(pieces, blocks, rows, spreading, start=None):
    width = pieces[0].shape[1]
    out_shape = (ROWS, len(blocks) * BLOCK) if spreading else (ROWS, width)
    inputs = [rows, *map(in_hbm, pieces)] + ([] if start is None else [start])
    specs = [pl.BlockSpec(memory_space=pltpu.HBM)] * len(pieces)
    specs = [whole(rows)] + specs + ([] if start is None else [whole(start)])
    return pl.pallas_call(
        functools.partial(
            stream_kernel, blocks, len(pieces), spreading, 0 if start is None else 1
        ),
        grid=(1,),
        in_specs=specs,
        out_specs=pl.BlockSpec(out_shape, lambda i: (0, 0)),
        out_shape=jax.ShapeDtypeStruct(out_shape, BF if spreading else F32),
        scratch_shapes=[
            pltpu.VMEM((DEPTH, BLOCK, width), BF),
            pltpu.SemaphoreType.DMA((DEPTH,)),
        ],
        compiler_params=pltpu.CompilerParams(vmem_limit_bytes=VMEM_LIMIT),
        cost_estimate=pl.CostEstimate(
            flops=32 * width * BLOCK * len(blocks),
            bytes_accessed=2 * width * BLOCK * len(blocks),
            transcendentals=0,
        ),
    )(*inputs)


def after(x, *others):
    return lax.optimization_barrier((x, *others))[0]


def body(rhs, lower_factor_tiles, tile_rows, diag_inv, inner_block, lower_row_solution):
    _, cases, width = rhs.shape
    group = lax.axis_index("grp")
    inverse, coupling = diag_inv[0], inner_block[0]
    per_panel = width // TILE
    chain_tiles = GROUPS * per_panel
    lower_tiles = lower_row_solution.shape[1] // TILE
    tile_count = chain_tiles + lower_tiles
    rows_shape = lambda dtype, panels=1: jax.ShapeDtypeStruct((ROWS, panels * width), dtype)

    def grow(x):
        return jnp.pad(x, ((0, ROWS - cases), (0, 0)))

    def hop(x, source, target):
        return lax.ppermute(x, "grp", [(source, target)])

    factor = lax.all_gather(lower_factor_tiles[0], "blk", axis=0, tiled=True)
    slot_rows = tile_rows[0, 0]
    slot_count = slot_rows.shape[0]
    places = [(0, slot * TILE) for slot in range(slot_count)]

    first = (group + 1) * per_panel
    near_tiles = (GROUPS - 1) * per_panel
    targets = jnp.where(slot_rows < chain_tiles, slot_rows - first, -1)
    numbers = jnp.arange(near_tiles, dtype=jnp.int32)
    missing = jnp.all(targets[None, :] != numbers[:, None], axis=1).astype(jnp.int32)
    low_numbers = jnp.arange(chain_tiles, tile_count, dtype=jnp.int32)
    low_numbers = jnp.roll(low_numbers.reshape(GROUPS, -1), -group, axis=0).reshape(-1)
    here = slot_rows[None, :] == low_numbers[:, None]
    slot_numbers = jnp.arange(slot_count, dtype=jnp.int32)
    turned = jnp.min(jnp.where(here, slot_numbers[None, :], slot_count), axis=1)
    low_index = jnp.where(
        (slot_rows >= chain_tiles) & (slot_rows < tile_count), slot_rows - chain_tiles, lower_tiles
    )
    low_rows = grow(lower_row_solution).reshape(ROWS, lower_tiles, TILE)
    low_rows = jnp.pad(low_rows, ((0, 0), (0, 1), (0, 0)))[:, low_index, :]
    low_rows = low_rows.reshape(ROWS, slot_count * TILE)

    acc = grow(rhs[0]).astype(F32)
    (solved,) = step_call(first_kernel, None, 0, [acc, inverse, coupling], [rows_shape(BF)])
    near, message = build([factor], places, targets, missing, solved)

    received = hop(message, 0, 1)
    blocks = [(0, n * BLOCK) for n in range(slot_count * TILE // BLOCK)]
    split = len(blocks) // 2
    owed = stream([factor], blocks[:split], low_rows[:, : split * BLOCK], False)
    for step in (1, 2):
        panels = GROUPS - 1 - step
        acc, solved, message = step_call(
            forward_kernel, near, panels, [after(acc, owed), inverse, coupling, received],
            [rows_shape(F32), rows_shape(BF), rows_shape(BF, panels)],
        )
        received = hop(message, step, step + 1)
        if step == 1:
            owed = stream([factor], blocks[split:], low_rows[:, split * BLOCK :], False, owed)
    solved, acc, message = step_call(
        turn_kernel, None, 0, [acc, owed, inverse, coupling, received],
        [rows_shape(BF), rows_shape(F32), rows_shape(BF)],
    )

    received = hop(message, 3, 2)
    beyond = [stream([factor], blocks[:split], solved, True)]
    acc, message = step_call(
        backward_kernel, near, 1, [after(acc, *beyond), inverse, coupling, received],
        [rows_shape(F32), rows_shape(BF, 2)],
    )
    received = hop(message, 2, 1)
    beyond.append(stream([factor], blocks[split:], after(solved, message), True))
    acc, message = step_call(
        backward_kernel, near, 2, [after(acc, *beyond), inverse, coupling, received],
        [rows_shape(F32), rows_shape(BF, 3)],
    )
    received = hop(message, 1, 0)
    beyond = after(jnp.concatenate(beyond, axis=1), message)[:cases].reshape(cases, slot_count, TILE)
    beyond = jnp.pad(beyond, ((0, 0), (0, 1), (0, 0)))[:, turned, :]
    beyond = beyond.reshape(cases, lower_tiles * TILE)
    beyond = after(beyond, received)
    part = lower_tiles * TILE // GROUPS
    parts = [beyond[:, :part]] + [
        lax.ppermute(
            beyond[:, shift * part : (shift + 1) * part],
            "grp",
            [(g, (g + shift) % GROUPS) for g in range(GROUPS)],
        )
        for shift in range(1, GROUPS)
    ]
    acc, settled = step_call(
        backward_kernel, near, 3, [acc, inverse, coupling, received],
        [rows_shape(F32), rows_shape(BF)],
    )
    pending = sum(p.astype(F32) for p in parts)
    return (solved[None, :cases], pending, settled[None, :cases])


def solution(mesh):
    placed = (
        P(None, "blk", "grp"),
        P(None, ("grp", "blk"), None),
        P(None, "grp", None),
        P(None, "grp", None),
        P(None, "grp", None),
        P("blk", None),
    )
    return jax.shard_map(
        body,
        mesh=mesh,
        in_specs=placed,
        out_specs=(P(None, "blk", "grp"), P("blk", "grp"), P(None, "blk", "grp")),
        check_vma=False,
    )
```

```python
import functools

import jax
import jax.numpy as jnp
from jax import lax
from jax.experimental import pallas as pl
from jax.experimental.pallas import tpu as pltpu
from jax.sharding import PartitionSpec as P

TILE = 64
GROUPS = 4
ROWS = 16
GROUP_ROWS = 1024
PARTS = 4
SIZE_Z, SIZE_X, CORES = 8, 4, 2
BF = jnp.bfloat16
F32 = jnp.float32
VMEM_LIMIT = 20 * 1024 * 1024
NT = (((1,), (1,)), ((), ()))


def mm(a, b):
    return jnp.dot(a, b, preferred_element_type=F32)


def mm_nt(a, b):
    return lax.dot_general(a, b, NT, preferred_element_type=F32)


def split_mm(product, r, w):
    high = r.astype(BF).astype(F32)
    both = product(jnp.concatenate([high, r - high], axis=0).astype(BF), w)
    return both[: r.shape[0]] + both[r.shape[0] :]


def lower_solve(residue, inverse, coupling):
    half = coupling.shape[0]
    leading = split_mm(mm, residue[:, :half], inverse[:half]).astype(BF)
    carried = residue[:, half:] - mm(leading, coupling[...])
    second = split_mm(mm, carried, inverse[half:]).astype(BF)
    return leading, second


def upper_solve(residue, inverse, coupling):
    half = coupling.shape[0]
    second = split_mm(mm_nt, residue[:, half:], inverse[half:]).astype(BF)
    carried = residue[:, :half] - mm_nt(second, coupling[...])
    return split_mm(mm_nt, carried, inverse[:half]).astype(BF), second


def store_halves(out, leading, second):
    half = leading.shape[1]
    out[:, :half] = leading.astype(out.dtype)
    out[:, half : 2 * half] = second.astype(out.dtype)


def first_kernel(acc, inverse, coupling, solved_out):
    store_halves(solved_out, *lower_solve(acc[...], inverse, coupling))


def build_kernel(places, count, targets, missing, *rest):
    pieces, solved = rest[:count], rest[count]
    *near_out, message_out, tiles, sems, out_sems = rest[count + 1 :]
    width = tiles.shape[1]

    def copy(slot):
        piece, start = places[slot]
        to = pl.multiple_of(jnp.maximum(targets[slot], 0) * TILE, TILE)
        return pltpu.make_async_copy(
            pieces[piece].at[pl.ds(start, TILE)], tiles.at[pl.ds(to, TILE)], sems.at[slot]
        )

    for slot in range(len(places)):

        @pl.when(targets[slot] >= 0)
        def _(slot=slot):
            copy(slot).start()

    for i in range(tiles.shape[0] // TILE):

        @pl.when(missing[i] > 0)
        def _(i=i):
            tiles[i * TILE : (i + 1) * TILE, :] = jnp.zeros((TILE, width), BF)

    for slot in range(len(places)):

        @pl.when(targets[slot] >= 0)
        def _(slot=slot):
            copy(slot).wait()

    kept = []
    for n in range(tiles.shape[0] // width):
        part = pl.ds(n * width, width)
        kept.append(pltpu.make_async_copy(tiles.at[part], near_out[n], out_sems.at[n]))
        kept[-1].start()
    for n in range(tiles.shape[0] // width):
        part = slice(n * width, (n + 1) * width)
        message_out[:, part] = mm_nt(solved[...], tiles[part, :]).astype(BF)
    for copy_out in kept:
        copy_out.wait()


def in_hbm(x):
    return pltpu.with_memory_space_constraint(x, pltpu.HBM)


def build(pieces, places, targets, missing, solved):
    width = solved.shape[1]
    near_rows = missing.shape[0] * TILE
    anywhere = pl.BlockSpec(memory_space=pl.ANY)
    held = pl.BlockSpec(memory_space=pltpu.HBM)
    return pl.pallas_call(
        functools.partial(build_kernel, places, len(pieces)),
        grid_spec=pltpu.PrefetchScalarGridSpec(
            num_scalar_prefetch=2,
            grid=(1,),
            in_specs=[held] * len(pieces) + [whole(solved)],
            out_specs=[anywhere] * (near_rows // width)
            + [pl.BlockSpec((ROWS, near_rows), lambda i, *_: (0, 0))],
            scratch_shapes=[
                pltpu.VMEM((near_rows, width), BF),
                pltpu.SemaphoreType.DMA((len(places),)),
                pltpu.SemaphoreType.DMA((near_rows // width,)),
            ],
        ),
        out_shape=[jax.ShapeDtypeStruct((width, width), BF)]
        + [pltpu.HBM((width, width), BF)] * (near_rows // width - 1)
        + [jax.ShapeDtypeStruct((ROWS, near_rows), BF)],
        compiler_params=pltpu.CompilerParams(vmem_limit_bytes=VMEM_LIMIT),
        cost_estimate=pl.CostEstimate(
            flops=300 * width * width, bytes_accessed=15 * width * width, transcendentals=0
        ),
    )(targets, missing, *map(in_hbm, pieces), solved)


def loads(sources, targets):
    groups = []
    sems = targets.pop() if sources else None
    for n, (source, target) in enumerate(zip(sources, targets)):
        rows = source.shape[0] // PARTS
        groups.append([])
        for i in range(PARTS):
            part = pl.ds(i * rows, rows)
            copy = pltpu.make_async_copy(source.at[part], target.at[part], sems.at[n * PARTS + i])
            copy.start()
            groups[-1].append(copy)

    def wait():
        for copy in groups.pop(0):
            copy.wait()

    return wait


def forward_kernel(panels, *rest):
    near, (first, acc, received, inverse, coupling) = rest[:panels], rest[panels : panels + 5]
    acc_out, solved_out, message_out, *tiles = rest[panels + 5 :]
    wait = loads(near, tiles)
    tiles = [first, *tiles]
    width = acc.shape[1]
    residue = acc[...] - received[:, :width].astype(F32)
    acc_out[...] = residue
    store_halves(solved_out, *lower_solve(residue, inverse, coupling))
    for n in range(panels + 1):
        if n:
            wait()
        product = mm_nt(solved_out[...], tiles[n][...])
        passed = received[:, (n + 1) * width : (n + 2) * width].astype(F32)
        message_out[:, n * width : (n + 1) * width] = (product + passed).astype(BF)


def turn_kernel(acc, received, owed, inverse, coupling, solved_out, residue_out, message_out):
    residue = acc[...] - received[...].astype(F32)
    store_halves(solved_out, *lower_solve(residue, inverse, coupling))
    residue = solved_out[...].astype(F32) - owed[...]
    residue_out[...] = residue
    store_halves(message_out, *upper_solve(residue, inverse, coupling))


def backward_kernel(panels, *rest):
    near, (first, acc, received, inverse, coupling) = rest[:panels], rest[panels : panels + 5]
    acc_out, message_out, *tiles = rest[panels + 5 :]
    wait = loads(near, tiles)
    tiles = [first, *tiles]
    width = acc.shape[1]
    if message_out.shape[1] > width:
        message_out[:, width:] = received[...]
    residue = acc[...]
    for n in range(panels + 1):
        if n:
            wait()
        residue = residue - mm(received[:, n * width : (n + 1) * width], tiles[n][...])
    acc_out[...] = residue
    store_halves(message_out, *upper_solve(residue, inverse, coupling))


def whole(x):
    return pl.BlockSpec(x.shape, lambda i, *_: (0,) * len(x.shape))


def step_call(kernel, near, operands, out_shapes):
    width = out_shapes[0].shape[1]
    count = len(near)
    return pl.pallas_call(
        kernel if kernel in (first_kernel, turn_kernel) else functools.partial(kernel, count),
        grid=(1,),
        in_specs=[pl.BlockSpec(memory_space=pltpu.HBM)] * count + [whole(x) for x in operands],
        out_specs=[whole(x) for x in out_shapes],
        out_shape=out_shapes,
        scratch_shapes=[pltpu.VMEM(x.shape, x.dtype) for x in near]
        + ([pltpu.SemaphoreType.DMA((count * PARTS,))] if near else []),
        compiler_params=pltpu.CompilerParams(vmem_limit_bytes=VMEM_LIMIT),
        cost_estimate=pl.CostEstimate(
            flops=100 * width * width, bytes_accessed=5 * width * width, transcendentals=0
        ),
    )(*map(in_hbm, near), *operands)


def streamed(heights, pieces, held, sems):
    copies, at = [], 0
    for n, height in enumerate(heights):
        target = held.at[pl.ds(at, height)]
        copies.append(pltpu.make_async_copy(pieces[n], target, sems.at[n]))
        copies[n].start()
        at += height
    first = at = 0
    for n, height in enumerate(heights):
        copies[n].wait()
        at += height
        if at - first >= GROUP_ROWS or n == len(heights) - 1:
            yield slice(first, at)
            first = at


def collect_kernel(heights, rows, *rest, started):
    count = len(heights)
    out, held, sems = rest[count + started :]
    total = rest[count][...] if started else None
    for here in streamed(heights, rest[:count], held, sems):
        product = mm(rows[:, here], held[here, :])
        total = product if total is None else total + product
    out[...] = total


def spread_kernel(heights, solved, *rest):
    count = len(heights)
    out, held, sems = rest[count:]
    for here in streamed(heights, rest[:count], held, sems):
        out[:, here] = mm_nt(solved[...], held[here, :])


def arrange_kernel(heights, order, solved, before, *rest):
    count = len(heights)
    out, held, products, sems = rest[count:]
    done = before.shape[1]
    products[:, :done] = before[...]
    for here in streamed(heights, rest[:count], held, sems):
        products[:, done + here.start : done + here.stop] = mm_nt(solved[...], held[here, :])
    lanes = 2 * TILE
    right = lax.broadcasted_iota(jnp.int32, (ROWS, lanes), 1) >= TILE
    slots = products.shape[1] // TILE

    def half(n, want):
        slot = order[n]
        held_at = jnp.minimum(slot, slots - 1)
        start = pl.multiple_of(lax.shift_right_logical(held_at, 1) * lanes, lanes)
        pair = products[:, pl.ds(start, lanes)]
        turned = jnp.where((held_at & 1) == want, pair, pltpu.roll(pair, TILE, 1))
        return jnp.where(slot < slots, turned, 0.0)

    for n in range(0, out.shape[1] // TILE, 2):
        both = jnp.where(right, half(n + 1, 1), half(n, 0))
        out[:, n * TILE : (n + 2) * TILE] = both.astype(BF)


def stream(kernel, pieces, operands, out_shape, tables=(), started=()):
    width = pieces[0].shape[1]
    heights = [p.shape[0] for p in pieces]
    total = sum(heights)
    inputs = [*operands, *map(in_hbm, pieces), *started]
    specs = [whole(x) for x in operands]
    specs += [pl.BlockSpec(memory_space=pltpu.HBM)] * len(pieces) + [whole(x) for x in started]
    scratch = [pltpu.VMEM((total, width), BF)]
    if tables:
        scratch.append(pltpu.VMEM(out_shape.shape, F32))
    return pl.pallas_call(
        functools.partial(kernel, heights),
        grid_spec=pltpu.PrefetchScalarGridSpec(
            num_scalar_prefetch=len(tables),
            grid=(1,),
            in_specs=specs,
            out_specs=whole(out_shape),
            scratch_shapes=scratch + [pltpu.SemaphoreType.DMA((len(pieces),))],
        ),
        out_shape=out_shape,
        compiler_params=pltpu.CompilerParams(vmem_limit_bytes=VMEM_LIMIT),
        cost_estimate=pl.CostEstimate(
            flops=32 * width * total, bytes_accessed=2 * width * total, transcendentals=0
        ),
    )(*tables, *inputs)


def after(x, *others):
    return lax.optimization_barrier((x, *others))[0]


class Block:
    def __init__(self, array, tags):
        self.array, self.tags = array, tags

    def head(self, tiles):
        return Block(None if self.array is None else self.array[: tiles * TILE], self.tags[:tiles])

    def tail(self, tiles):
        return Block(None if self.array is None else self.array[tiles * TILE :], self.tags[tiles:])

    def after(self, *others):
        others = [o.array if isinstance(o, Block) else o for o in others]
        return Block(None if self.array is None else after(self.array, *others), self.tags)


def joined(*blocks):
    arrays = [b.array for b in blocks]
    array = None if arrays[0] is None else jnp.concatenate(arrays, axis=0)
    return Block(array, [t for b in blocks for t in b.tags])


def blk_index(z, x, c):
    return ((z % SIZE_Z) * SIZE_X + x % SIZE_X) * CORES + c


def blk_permute(array, target):
    pairs = [
        (blk_index(z, x, c), blk_index(*target(z, x, c)))
        for z in range(SIZE_Z)
        for x in range(SIZE_X)
        for c in range(CORES)
    ]
    return None if array is None else lax.ppermute(array, "blk", pairs)


def ring_z(block):
    array = blk_permute(block.array, lambda z, x, c: (z + 1 - 2 * c, x, c))
    return Block(array, [(dz + 1, dx, f, t) for dz, dx, f, t in block.tags])


def ring_x(block):
    array = blk_permute(block.array, lambda z, x, c: (z, x + 1 - 2 * c, c))
    return Block(array, [(dz, dx + 1, f, t) for dz, dx, f, t in block.tags])


def swap(block):
    array = blk_permute(block.array, lambda z, x, c: (z, x, 1 - c))
    return Block(array, [(-dz, -dx, 1 - f, t) for dz, dx, f, t in block.tags])


def gather_plane(own, beside):
    own = Block(own, [(0, 0, 0, 0), (0, 0, 0, 1)])
    other = swap(own)
    b = joined(own.tail(1), other.tail(1))
    a = joined(own.head(1), other.head(1))
    b_x = ring_x(b)
    a_1 = ring_z(a)
    n_1 = ring_z(b)
    b_far = ring_x(b_x.head(1))
    a_2 = ring_z(a_1)
    n_2 = ring_z(n_1)
    left = joined(b_x, b_far)
    l1 = ring_z(left)
    right = swap(left)
    a_3 = ring_z(a_2)
    early = joined(own.head(1), a_1, a_2)
    early_x = ring_x(early)
    m1 = ring_z(right)
    early_s = swap(early)
    n_3 = ring_z(n_2)
    early_sx = ring_x(early_s)
    l2 = ring_z(l1.after(early_s))
    s_l1 = swap(l1)
    a_4 = ring_z(a_3.head(1))
    early_far = ring_x(early_x.after(s_l1))
    s_early_x = swap(early_x)
    m2 = ring_z(m1)
    s_m1 = swap(m1)
    n_4 = ring_z(n_3.head(1).after(s_early_x))
    s_early_sx = swap(early_sx.after(n_3, s_m1))
    l3 = ring_z(l2.after(early_sx))
    s_l2 = swap(l2)
    late = joined(a_3, a_4)
    late_x = ring_x(late.after(s_early_sx, *beside))
    late_s = swap(late)
    late_sx = ring_x(late_s.after(s_l2))
    s_early_far = swap(early_far.after(late_s))
    m3 = ring_z(m2)
    s_m2 = swap(m2)
    n_all = joined(n_1, n_2, n_3, n_4)
    s_n = swap(n_all)
    late_far = ring_x(late_x.after(s_early_far, s_m2))
    s_late_x = swap(late_x)
    l4 = ring_z(l3.after(s_n))
    s_l3 = swap(l3)
    s_late_sx = swap(late_sx.after(s_late_x))
    s_m3 = swap(m3.after(s_l3))
    s_late_far = swap(late_far.after(s_late_sx, s_m3))
    s_l4 = swap(l4)
    blocks = [early, early_s, late, late_s, left, right, b, n_all, early_x, l1, m1, early_sx, l2, m2,
        early_far, late_x, l3, m3, late_sx, late_far, l4, s_n, s_early_x, s_l1, s_m1, s_early_sx, s_l2, s_m2,
        s_early_far, s_late_x, s_l3, s_m3, s_late_sx, s_late_far, s_l4]
    return blocks


def body(rhs, lower_factor_tiles, tile_rows, diag_inv, inner_block, lower_row_solution):
    _, cases, width = rhs.shape
    group = lax.axis_index("grp")
    inverse, coupling = diag_inv[0], inner_block[0]
    per_panel = width // TILE
    chain_tiles = GROUPS * per_panel
    lower_tiles = lower_row_solution.shape[1] // TILE
    tile_count = chain_tiles + lower_tiles
    rows_shape = lambda dtype, panels=1: jax.ShapeDtypeStruct((ROWS, panels * width), dtype)

    def grow(x):
        return jnp.pad(x, ((0, ROWS - cases), (0, 0)))

    def hop(x, source, target):
        return lax.ppermute(x, "grp", [(source, target)])

    def gathered(own, *beside):
        blocks = sorted(gather_plane(own, beside), key=lambda b: len(b.tags))
        return blocks[0::2] + blocks[1::2]

    blocks = gathered(None)
    places = [(n, i * TILE) for n, b in enumerate(blocks) for i in range(len(b.tags))]
    tags = [tag for b in blocks for tag in b.tags]
    slot_count = len(tags)
    split = len(blocks) // 2
    split_rows = sum(len(b.tags) for b in blocks[:split]) * TILE
    place_index = lax.axis_index("blk")
    core = place_index % CORES
    sign = 2 * core - 1
    dz, dx, flip, tile = (jnp.asarray(column, jnp.int32) for column in zip(*tags))
    source_z = (place_index // (SIZE_X * CORES) + sign * dz) % SIZE_Z
    source_x = (place_index // CORES + sign * dx) % SIZE_X
    source = (source_z * SIZE_X + source_x) * CORES + (core + flip) % CORES
    per_device = lower_factor_tiles.shape[1] // TILE
    slot_rows = tile_rows[0, 0][source * per_device + tile]

    first = (group + 1) * per_panel
    near_tiles = (GROUPS - 1) * per_panel
    targets = jnp.where(slot_rows < chain_tiles, slot_rows - first, -1)
    numbers = jnp.arange(near_tiles, dtype=jnp.int32)
    missing = jnp.all(targets[None, :] != numbers[:, None], axis=1).astype(jnp.int32)
    low_numbers = jnp.arange(chain_tiles, tile_count, dtype=jnp.int32)
    low_numbers = jnp.roll(low_numbers.reshape(GROUPS, -1), -group, axis=0).reshape(-1)
    here = slot_rows[None, :] == low_numbers[:, None]
    slot_numbers = jnp.arange(slot_count, dtype=jnp.int32)
    turned = jnp.min(jnp.where(here, slot_numbers[None, :], slot_count), axis=1)
    low_index = jnp.where(
        (slot_rows >= chain_tiles) & (slot_rows < tile_count), slot_rows - chain_tiles, lower_tiles
    )
    low_rows = grow(lower_row_solution).reshape(ROWS, lower_tiles, TILE)
    low_rows = jnp.pad(low_rows, ((0, 0), (0, 1), (0, 0)))[:, low_index, :]
    low_rows = low_rows.reshape(ROWS, slot_count * TILE)

    acc = grow(rhs[0]).astype(F32)
    (solved,) = step_call(first_kernel, [], [acc, inverse, coupling], [rows_shape(BF)])
    pieces = [
        b.array for b in gathered(lower_factor_tiles[0], solved, low_rows, targets, missing, turned)
    ]
    *near, message = build(pieces, places, targets, missing, solved)

    received = hop(message, 0, 1)
    owed = stream(
        functools.partial(collect_kernel, started=0), pieces[:split], [low_rows[:, :split_rows]],
        rows_shape(F32),
    )
    for step in (1, 2):
        panels = GROUPS - 1 - step
        acc, solved, message = step_call(
            forward_kernel, near[1:panels], [near[0], after(acc, owed), received, inverse, coupling],
            [rows_shape(F32), rows_shape(BF), rows_shape(BF, panels)],
        )
        received = hop(message, step, step + 1)
        if step == 1:
            owed = stream(
                functools.partial(collect_kernel, started=1), pieces[split:],
                [low_rows[:, split_rows:]], rows_shape(F32), started=[owed],
            )
    solved, acc, message = step_call(
        turn_kernel, [], [acc, received, owed, inverse, coupling],
        [rows_shape(BF), rows_shape(F32), rows_shape(BF)],
    )

    received = hop(message, 3, 2)
    beyond = stream(
        spread_kernel, pieces[:split], [solved], jax.ShapeDtypeStruct((ROWS, split_rows), F32)
    )
    acc, message = step_call(
        backward_kernel, near[1:1], [near[0], after(acc, beyond), received, inverse, coupling],
        [rows_shape(F32), rows_shape(BF, 2)],
    )
    received = hop(message, 2, 1)
    beyond = stream(
        arrange_kernel, pieces[split:], [after(solved, message), beyond],
        jax.ShapeDtypeStruct((ROWS, lower_tiles * TILE), BF), [turned],
    )
    acc, message = step_call(
        backward_kernel, near[1:2], [near[0], after(acc, beyond), received, inverse, coupling],
        [rows_shape(F32), rows_shape(BF, 3)],
    )
    received = hop(message, 1, 0)
    beyond = beyond[:cases]
    beyond = after(beyond, received)
    part = lower_tiles * TILE // GROUPS
    parts = [beyond[:, :part]] + [
        lax.ppermute(
            beyond[:, shift * part : (shift + 1) * part],
            "grp",
            [(g, (g + shift) % GROUPS) for g in range(GROUPS)],
        )
        for shift in range(1, GROUPS)
    ]
    acc, settled = step_call(
        backward_kernel, near[1:], [near[0], acc, received, inverse, coupling],
        [rows_shape(F32), rows_shape(BF)],
    )
    pending = sum(p.astype(F32) for p in parts)
    return (solved[None, :cases], pending, settled[None, :cases])


def solution(mesh):
    placed = (
        P(None, "blk", "grp"),
        P(None, ("grp", "blk"), None),
        P(None, "grp", None),
        P(None, "grp", None),
        P(None, "grp", None),
        P("blk", None),
    )
    return jax.shard_map(
        body,
        mesh=mesh,
        in_specs=placed,
        out_specs=(P(None, "blk", "grp"), P("blk", "grp"), P(None, "blk", "grp")),
        check_vma=False,
    )
```

```python
import functools

import jax
import jax.numpy as jnp
from jax import lax
from jax.experimental import pallas as pl
from jax.experimental.pallas import tpu as pltpu
from jax.sharding import PartitionSpec as P

TILE = 64
GROUPS = 4
ROWS = 16
GROUP_ROWS = 1024
PARTS = 4
SIZE_Z, SIZE_X, CORES = 8, 4, 2
BF = jnp.bfloat16
F32 = jnp.float32
VMEM_LIMIT = 20 * 1024 * 1024
NT = (((1,), (1,)), ((), ()))


def mm(a, b):
    return jnp.dot(a, b, preferred_element_type=F32)


def mm_nt(a, b):
    return lax.dot_general(a, b, NT, preferred_element_type=F32)


def split_mm(product, r, w):
    high = r.astype(BF).astype(F32)
    both = product(jnp.concatenate([high, r - high], axis=0).astype(BF), w)
    return both[: r.shape[0]] + both[r.shape[0] :]


def lower_solve(residue, inverse, coupling):
    half = coupling.shape[0]
    leading = split_mm(mm, residue[:, :half], inverse[:half]).astype(BF)
    carried = residue[:, half:] - mm(leading, coupling[...])
    second = split_mm(mm, carried, inverse[half:]).astype(BF)
    return leading, second


def upper_solve(residue, inverse, coupling):
    half = coupling.shape[0]
    second = split_mm(mm_nt, residue[:, half:], inverse[half:]).astype(BF)
    carried = residue[:, :half] - mm_nt(second, coupling[...])
    return split_mm(mm_nt, carried, inverse[:half]).astype(BF), second


def store_halves(out, leading, second):
    half = leading.shape[1]
    out[:, :half] = leading.astype(out.dtype)
    out[:, half : 2 * half] = second.astype(out.dtype)


def first_kernel(acc, inverse, coupling, solved_out):
    store_halves(solved_out, *lower_solve(acc[...], inverse, coupling))


def build_kernel(places, count, targets, missing, *rest):
    pieces, solved = rest[:count], rest[count]
    *near_out, message_out, tiles, sems, out_sems = rest[count + 1 :]
    width = tiles.shape[1]

    def copy(slot):
        piece, start = places[slot]
        to = pl.multiple_of(jnp.maximum(targets[slot], 0) * TILE, TILE)
        return pltpu.make_async_copy(
            pieces[piece].at[pl.ds(start, TILE)], tiles.at[pl.ds(to, TILE)], sems.at[slot]
        )

    for slot in range(len(places)):

        @pl.when(targets[slot] >= 0)
        def _(slot=slot):
            copy(slot).start()

    for i in range(tiles.shape[0] // TILE):

        @pl.when(missing[i] > 0)
        def _(i=i):
            tiles[i * TILE : (i + 1) * TILE, :] = jnp.zeros((TILE, width), BF)

    for slot in range(len(places)):

        @pl.when(targets[slot] >= 0)
        def _(slot=slot):
            copy(slot).wait()

    kept = []
    for n in range(tiles.shape[0] // width):
        part = pl.ds(n * width, width)
        kept.append(pltpu.make_async_copy(tiles.at[part], near_out[n], out_sems.at[n]))
        kept[-1].start()
    for n in range(tiles.shape[0] // width):
        part = slice(n * width, (n + 1) * width)
        message_out[:, part] = mm_nt(solved[...], tiles[part, :]).astype(BF)
    for copy_out in kept:
        copy_out.wait()


def in_hbm(x):
    return pltpu.with_memory_space_constraint(x, pltpu.HBM)


def build(pieces, places, targets, missing, solved):
    width = solved.shape[1]
    near_rows = missing.shape[0] * TILE
    anywhere = pl.BlockSpec(memory_space=pl.ANY)
    held = pl.BlockSpec(memory_space=pltpu.HBM)
    return pl.pallas_call(
        functools.partial(build_kernel, places, len(pieces)),
        grid_spec=pltpu.PrefetchScalarGridSpec(
            num_scalar_prefetch=2,
            grid=(1,),
            in_specs=[held] * len(pieces) + [whole(solved)],
            out_specs=[anywhere] * (near_rows // width)
            + [pl.BlockSpec((ROWS, near_rows), lambda i, *_: (0, 0))],
            scratch_shapes=[
                pltpu.VMEM((near_rows, width), BF),
                pltpu.SemaphoreType.DMA((len(places),)),
                pltpu.SemaphoreType.DMA((near_rows // width,)),
            ],
        ),
        out_shape=[jax.ShapeDtypeStruct((width, width), BF)]
        + [pltpu.HBM((width, width), BF)] * (near_rows // width - 1)
        + [jax.ShapeDtypeStruct((ROWS, near_rows), BF)],
        compiler_params=pltpu.CompilerParams(vmem_limit_bytes=VMEM_LIMIT),
        cost_estimate=pl.CostEstimate(
            flops=300 * width * width, bytes_accessed=15 * width * width, transcendentals=0
        ),
    )(targets, missing, *map(in_hbm, pieces), solved)


def loads(sources, targets):
    groups = []
    sems = targets.pop() if sources else None
    for n, (source, target) in enumerate(zip(sources, targets)):
        rows = source.shape[0] // PARTS
        groups.append([])
        for i in range(PARTS):
            part = pl.ds(i * rows, rows)
            copy = pltpu.make_async_copy(source.at[part], target.at[part], sems.at[n * PARTS + i])
            copy.start()
            groups[-1].append(copy)

    def wait():
        for copy in groups.pop(0):
            copy.wait()

    return wait


def forward_kernel(panels, resident, *rest):
    near, held = rest[:panels], rest[panels : panels + resident]
    acc, received, inverse, coupling, *rest = rest[panels + resident :]
    acc_out, solved_out, message_out, *tiles = rest
    wait = loads(near, tiles)
    tiles = [*held, *tiles]
    width = acc.shape[1]
    residue = acc[...] - received[:, :width].astype(F32)
    acc_out[...] = residue
    store_halves(solved_out, *lower_solve(residue, inverse, coupling))
    for n in range(resident + panels):
        if n >= resident:
            wait()
        product = mm_nt(solved_out[...], tiles[n][...])
        passed = received[:, (n + 1) * width : (n + 2) * width].astype(F32)
        message_out[:, n * width : (n + 1) * width] = (product + passed).astype(BF)


def turn_kernel(acc, received, owed, inverse, coupling, solved_out, residue_out, message_out):
    residue = acc[...] - received[...].astype(F32)
    store_halves(solved_out, *lower_solve(residue, inverse, coupling))
    residue = solved_out[...].astype(F32) - owed[...]
    residue_out[...] = residue
    store_halves(message_out, *upper_solve(residue, inverse, coupling))


def backward_kernel(panels, resident, *rest):
    near, held = rest[:panels], rest[panels : panels + resident]
    acc, received, inverse, coupling, *rest = rest[panels + resident :]
    acc_out, message_out, *tiles = rest
    wait = loads(near, tiles)
    tiles = [*held, *tiles]
    width = acc.shape[1]
    if message_out.shape[1] > width:
        message_out[:, width:] = received[...]
    residue = acc[...]
    for n in range(resident + panels):
        if n >= resident:
            wait()
        residue = residue - mm(received[:, n * width : (n + 1) * width], tiles[n][...])
    acc_out[...] = residue
    store_halves(message_out, *upper_solve(residue, inverse, coupling))


def whole(x):
    return pl.BlockSpec(x.shape, lambda i, *_: (0,) * len(x.shape))


def step_call(kernel, near, operands, out_shapes, resident=0):
    width = out_shapes[0].shape[1]
    count = len(near)
    return pl.pallas_call(
        functools.partial(kernel, count, resident) if resident else kernel,
        grid=(1,),
        in_specs=[pl.BlockSpec(memory_space=pltpu.HBM)] * count + [whole(x) for x in operands],
        out_specs=[whole(x) for x in out_shapes],
        out_shape=out_shapes,
        scratch_shapes=[pltpu.VMEM(x.shape, x.dtype) for x in near]
        + ([pltpu.SemaphoreType.DMA((count * PARTS,))] if near else []),
        compiler_params=pltpu.CompilerParams(vmem_limit_bytes=VMEM_LIMIT),
        cost_estimate=pl.CostEstimate(
            flops=100 * width * width, bytes_accessed=5 * width * width, transcendentals=0
        ),
    )(*map(in_hbm, near), *operands)


def streamed(heights, pieces, held, sems):
    copies, at = [], 0
    for n, height in enumerate(heights):
        target = held.at[pl.ds(at, height)]
        copies.append(pltpu.make_async_copy(pieces[n], target, sems.at[n]))
        copies[n].start()
        at += height
    first = at = 0
    for n, height in enumerate(heights):
        copies[n].wait()
        at += height
        if at - first >= GROUP_ROWS or n == len(heights) - 1:
            yield slice(first, at)
            first = at


def collect_kernel(heights, rows, *rest, started):
    count = len(heights)
    out, held, sems = rest[count + started :]
    total = rest[count][...] if started else None
    for here in streamed(heights, rest[:count], held, sems):
        product = mm(rows[:, here], held[here, :])
        total = product if total is None else total + product
    out[...] = total


def spread_kernel(heights, solved, *rest):
    count = len(heights)
    out, held, sems = rest[count:]
    for here in streamed(heights, rest[:count], held, sems):
        out[:, here] = mm_nt(solved[...], held[here, :])


def arrange_kernel(order, rows, out):
    lanes = 2 * TILE
    right = lax.broadcasted_iota(jnp.int32, (ROWS, lanes), 1) >= TILE
    tiles = rows.shape[1] // TILE

    def half(n, want):
        tile = order[n]
        held_at = jnp.minimum(tile, tiles - 1)
        start = pl.multiple_of(lax.shift_right_logical(held_at, 1) * lanes, lanes)
        pair = rows[:, pl.ds(start, lanes)]
        turned = jnp.where((held_at & 1) == want, pair, pltpu.roll(pair, TILE, 1))
        return jnp.where(tile < tiles, turned, 0.0)

    for n in range(0, out.shape[1] // TILE, 2):
        both = jnp.where(right, half(n + 1, 1), half(n, 0))
        out[:, n * TILE : (n + 2) * TILE] = both.astype(BF)


def arrange(order, rows):
    out_shape = jax.ShapeDtypeStruct((ROWS, order.shape[0] * TILE), BF)
    return pl.pallas_call(
        arrange_kernel,
        grid_spec=pltpu.PrefetchScalarGridSpec(
            num_scalar_prefetch=1,
            grid=(1,),
            in_specs=[whole(rows)],
            out_specs=whole(out_shape),
        ),
        out_shape=out_shape,
        compiler_params=pltpu.CompilerParams(vmem_limit_bytes=VMEM_LIMIT),
        cost_estimate=pl.CostEstimate(
            flops=50_000_000, bytes_accessed=4_000_000, transcendentals=0
        ),
    )(order, rows)


def stream(kernel, pieces, operands, out_shape, started=()):
    width = pieces[0].shape[1]
    heights = [p.shape[0] for p in pieces]
    total = sum(heights)
    inputs = [*operands, *map(in_hbm, pieces), *started]
    specs = [whole(x) for x in operands]
    specs += [pl.BlockSpec(memory_space=pltpu.HBM)] * len(pieces) + [whole(x) for x in started]
    return pl.pallas_call(
        functools.partial(kernel, heights),
        grid=(1,),
        in_specs=specs,
        out_specs=whole(out_shape),
        scratch_shapes=[
            pltpu.VMEM((total, width), BF),
            pltpu.SemaphoreType.DMA((len(pieces),)),
        ],
        out_shape=out_shape,
        compiler_params=pltpu.CompilerParams(vmem_limit_bytes=VMEM_LIMIT),
        cost_estimate=pl.CostEstimate(
            flops=32 * width * total, bytes_accessed=2 * width * total, transcendentals=0
        ),
    )(*inputs)


def after(x, *others):
    return lax.optimization_barrier((x, *others))[0]


class Block:
    def __init__(self, array, tags):
        self.array, self.tags = array, tags

    def head(self, tiles):
        return Block(None if self.array is None else self.array[: tiles * TILE], self.tags[:tiles])

    def tail(self, tiles):
        return Block(None if self.array is None else self.array[tiles * TILE :], self.tags[tiles:])

    def after(self, *others):
        others = [o.array if isinstance(o, Block) else o for o in others]
        return Block(None if self.array is None else after(self.array, *others), self.tags)


def joined(*blocks):
    arrays = [b.array for b in blocks]
    array = None if arrays[0] is None else jnp.concatenate(arrays, axis=0)
    return Block(array, [t for b in blocks for t in b.tags])


def blk_index(z, x, c):
    return ((z % SIZE_Z) * SIZE_X + x % SIZE_X) * CORES + c


def blk_permute(array, target):
    pairs = [
        (blk_index(z, x, c), blk_index(*target(z, x, c)))
        for z in range(SIZE_Z)
        for x in range(SIZE_X)
        for c in range(CORES)
    ]
    return None if array is None else lax.ppermute(array, "blk", pairs)


def ring_z(block):
    array = blk_permute(block.array, lambda z, x, c: (z + 1 - 2 * c, x, c))
    return Block(array, [(dz + 1, dx, f, t) for dz, dx, f, t in block.tags])


def ring_x(block):
    array = blk_permute(block.array, lambda z, x, c: (z, x + 1 - 2 * c, c))
    return Block(array, [(dz, dx + 1, f, t) for dz, dx, f, t in block.tags])


def swap(block):
    array = blk_permute(block.array, lambda z, x, c: (z, x, 1 - c))
    return Block(array, [(-dz, -dx, 1 - f, t) for dz, dx, f, t in block.tags])


def gather_plane(own, beside):
    own = Block(own, [(0, 0, 0, 0), (0, 0, 0, 1)])
    other = swap(own)
    b = joined(own.tail(1), other.tail(1))
    a = joined(own.head(1), other.head(1))
    b_x = ring_x(b)
    a_1 = ring_z(a)
    n_1 = ring_z(b)
    b_far = ring_x(b_x.head(1))
    a_2 = ring_z(a_1)
    n_2 = ring_z(n_1)
    left = joined(b_x, b_far)
    l1 = ring_z(left)
    right = swap(left)
    a_3 = ring_z(a_2)
    early = joined(own.head(1), a_1, a_2)
    early_x = ring_x(early)
    m1 = ring_z(right)
    early_s = swap(early)
    n_3 = ring_z(n_2)
    early_sx = ring_x(early_s)
    l2 = ring_z(l1.after(early_s))
    s_l1 = swap(l1)
    a_4 = ring_z(a_3.head(1))
    early_far = ring_x(early_x.after(s_l1))
    s_early_x = swap(early_x)
    m2 = ring_z(m1)
    s_m1 = swap(m1)
    n_4 = ring_z(n_3.head(1).after(s_early_x))
    s_early_sx = swap(early_sx.after(n_3, s_m1))
    l3 = ring_z(l2.after(early_sx))
    s_l2 = swap(l2)
    late = joined(a_3, a_4)
    late_x = ring_x(late.after(s_early_sx, *beside))
    late_s = swap(late)
    late_sx = ring_x(late_s.after(s_l2))
    s_early_far = swap(early_far.after(late_s))
    m3 = ring_z(m2)
    s_m2 = swap(m2)
    n_all = joined(n_1, n_2, n_3, n_4)
    s_n = swap(n_all)
    late_far = ring_x(late_x.after(s_early_far, s_m2))
    s_late_x = swap(late_x)
    l4 = ring_z(l3.after(s_n))
    s_l3 = swap(l3)
    s_late_sx = swap(late_sx.after(s_late_x))
    s_m3 = swap(m3.after(s_l3))
    s_late_far = swap(late_far.after(s_late_sx, s_m3))
    s_l4 = swap(l4)
    blocks = [early, early_s, late, late_s, left, right, b, n_all, early_x, l1, m1, early_sx, l2, m2,
        early_far, late_x, l3, m3, late_sx, late_far, l4, s_n, s_early_x, s_l1, s_m1, s_early_sx, s_l2, s_m2,
        s_early_far, s_late_x, s_l3, s_m3, s_late_sx, s_late_far, s_l4]
    return blocks


def body(rhs, lower_factor_tiles, tile_rows, diag_inv, inner_block, lower_row_solution):
    _, cases, width = rhs.shape
    group = lax.axis_index("grp")
    inverse, coupling = diag_inv[0], inner_block[0]
    per_panel = width // TILE
    chain_tiles = GROUPS * per_panel
    lower_tiles = lower_row_solution.shape[1] // TILE
    tile_count = chain_tiles + lower_tiles
    rows_shape = lambda dtype, panels=1: jax.ShapeDtypeStruct((ROWS, panels * width), dtype)

    def grow(x):
        return jnp.pad(x, ((0, ROWS - cases), (0, 0)))

    def hop(x, source, target):
        return lax.ppermute(x, "grp", [(source, target)])

    def gathered(own, *beside):
        blocks = sorted(gather_plane(own, beside), key=lambda b: len(b.tags))
        return blocks[0::2] + blocks[1::2]

    blocks = gathered(None)
    places = [(n, i * TILE) for n, b in enumerate(blocks) for i in range(len(b.tags))]
    tags = [tag for b in blocks for tag in b.tags]
    slot_count = len(tags)
    split = len(blocks) // 2
    split_rows = sum(len(b.tags) for b in blocks[:split]) * TILE
    place_index = lax.axis_index("blk")
    core = place_index % CORES
    sign = 2 * core - 1
    dz, dx, flip, tile = (jnp.asarray(column, jnp.int32) for column in zip(*tags))
    source_z = (place_index // (SIZE_X * CORES) + sign * dz) % SIZE_Z
    source_x = (place_index // CORES + sign * dx) % SIZE_X
    source = (source_z * SIZE_X + source_x) * CORES + (core + flip) % CORES
    per_device = lower_factor_tiles.shape[1] // TILE
    slot_rows = tile_rows[0, 0][source * per_device + tile]

    first = (group + 1) * per_panel
    near_tiles = (GROUPS - 1) * per_panel
    targets = jnp.where(slot_rows < chain_tiles, slot_rows - first, -1)
    numbers = jnp.arange(near_tiles, dtype=jnp.int32)
    missing = jnp.all(targets[None, :] != numbers[:, None], axis=1).astype(jnp.int32)
    low_numbers = jnp.arange(chain_tiles, tile_count, dtype=jnp.int32)
    low_numbers = jnp.roll(low_numbers.reshape(GROUPS, -1), -group, axis=0).reshape(-1)
    here = slot_rows[None, :] == low_numbers[:, None]
    slot_numbers = jnp.arange(slot_count, dtype=jnp.int32)
    turned = jnp.min(jnp.where(here, slot_numbers[None, :], slot_count), axis=1)
    low_index = jnp.where(
        (slot_rows >= chain_tiles) & (slot_rows < tile_count), slot_rows - chain_tiles, lower_tiles
    )
    low_rows = grow(lower_row_solution).reshape(ROWS, lower_tiles, TILE)
    low_rows = jnp.pad(low_rows, ((0, 0), (0, 1), (0, 0)))[:, low_index, :]
    low_rows = low_rows.reshape(ROWS, slot_count * TILE)

    acc = grow(rhs[0]).astype(F32)
    (solved,) = step_call(first_kernel, [], [acc, inverse, coupling], [rows_shape(BF)])
    pieces = [
        b.array for b in gathered(lower_factor_tiles[0], solved, low_rows, targets, missing, turned)
    ]
    *near, message = build(pieces, places, targets, missing, solved)

    received = hop(message, 0, 1)
    owed = stream(
        functools.partial(collect_kernel, started=0), pieces[:split], [low_rows[:, :split_rows]],
        rows_shape(F32),
    )
    for step in (1, 2):
        panels = GROUPS - 1 - step
        acc, solved, message = step_call(
            forward_kernel, [], [*near[:panels], after(acc, owed), received, inverse, coupling],
            [rows_shape(F32), rows_shape(BF), rows_shape(BF, panels)], panels,
        )
        received = hop(message, step, step + 1)
        if step == 1:
            owed = stream(
                functools.partial(collect_kernel, started=1), pieces[split:],
                [low_rows[:, split_rows:]], rows_shape(F32), started=[owed],
            )
    solved, acc, message = step_call(
        turn_kernel, [], [acc, received, owed, inverse, coupling],
        [rows_shape(BF), rows_shape(F32), rows_shape(BF)],
    )

    received = hop(message, 3, 2)
    beyond = [
        stream(
            spread_kernel, pieces[:split], [solved], jax.ShapeDtypeStruct((ROWS, split_rows), F32)
        )
    ]
    acc, message = step_call(
        backward_kernel, [], [near[0], after(acc, *beyond), received, inverse, coupling],
        [rows_shape(F32), rows_shape(BF, 2)], 1,
    )
    received = hop(message, 2, 1)
    beyond.append(
        stream(
            spread_kernel, pieces[split:], [after(solved, message)],
            jax.ShapeDtypeStruct((ROWS, slot_count * TILE - split_rows), F32),
        )
    )
    acc, message = step_call(
        backward_kernel, [], [*near[:2], after(acc, *beyond), received, inverse, coupling],
        [rows_shape(F32), rows_shape(BF, 3)], 2,
    )
    received = hop(message, 1, 0)
    beyond = arrange(turned, after(jnp.concatenate(beyond, axis=1), message))[:cases]
    beyond = after(beyond, received)
    part = lower_tiles * TILE // GROUPS
    parts = [beyond[:, :part]] + [
        lax.ppermute(
            beyond[:, shift * part : (shift + 1) * part],
            "grp",
            [(g, (g + shift) % GROUPS) for g in range(GROUPS)],
        )
        for shift in range(1, GROUPS)
    ]
    acc, settled = step_call(
        backward_kernel, near[2:], [*near[:2], acc, received, inverse, coupling],
        [rows_shape(F32), rows_shape(BF)], 2,
    )
    pending = sum(p.astype(F32) for p in parts)
    return (solved[None, :cases], pending, settled[None, :cases])


def solution(mesh):
    placed = (
        P(None, "blk", "grp"),
        P(None, ("grp", "blk"), None),
        P(None, "grp", None),
        P(None, "grp", None),
        P(None, "grp", None),
        P("blk", None),
    )
    return jax.shard_map(
        body,
        mesh=mesh,
        in_specs=placed,
        out_specs=(P(None, "blk", "grp"), P("blk", "grp"), P(None, "blk", "grp")),
        check_vma=False,
    )
```

```python
import functools

import jax
import jax.numpy as jnp
from jax import lax
from jax.experimental import pallas as pl
from jax.experimental.pallas import tpu as pltpu
from jax.sharding import PartitionSpec as P

TILE = 64
GROUPS = 4
ROWS = 16
GROUP_ROWS = 1024
PARTS = 4
SIZE_Z, SIZE_X, CORES = 8, 4, 2
BF = jnp.bfloat16
F32 = jnp.float32
VMEM_LIMIT = 20 * 1024 * 1024
NT = (((1,), (1,)), ((), ()))


def mm(a, b):
    return jnp.dot(a, b, preferred_element_type=F32)


def mm_nt(a, b):
    return lax.dot_general(a, b, NT, preferred_element_type=F32)


def split_mm(product, r, w):
    high = r.astype(BF).astype(F32)
    both = product(jnp.concatenate([high, r - high], axis=0).astype(BF), w)
    return both[: r.shape[0]] + both[r.shape[0] :]


def lower_solve(residue, inverse, coupling):
    half = coupling.shape[0]
    leading = split_mm(mm, residue[:, :half], inverse[:half]).astype(BF)
    carried = residue[:, half:] - mm(leading, coupling[...])
    second = split_mm(mm, carried, inverse[half:]).astype(BF)
    return leading, second


def upper_solve(residue, inverse, coupling):
    half = coupling.shape[0]
    second = split_mm(mm_nt, residue[:, half:], inverse[half:]).astype(BF)
    carried = residue[:, :half] - mm_nt(second, coupling[...])
    return split_mm(mm_nt, carried, inverse[:half]).astype(BF), second


def store_halves(out, leading, second):
    half = leading.shape[1]
    out[:, :half] = leading.astype(out.dtype)
    out[:, half : 2 * half] = second.astype(out.dtype)


def first_kernel(acc, inverse, coupling, solved_out):
    store_halves(solved_out, *lower_solve(acc[...], inverse, coupling))


def build_kernel(places, count, targets, missing, *rest):
    pieces, solved = rest[:count], rest[count]
    *near_out, message_out, tiles, sems, out_sems = rest[count + 1 :]
    width = tiles.shape[1]

    def copy(slot):
        piece, start = places[slot]
        to = pl.multiple_of(jnp.maximum(targets[slot], 0) * TILE, TILE)
        return pltpu.make_async_copy(
            pieces[piece].at[pl.ds(start, TILE)], tiles.at[pl.ds(to, TILE)], sems.at[slot]
        )

    for slot in range(len(places)):

        @pl.when(targets[slot] >= 0)
        def _(slot=slot):
            copy(slot).start()

    for i in range(tiles.shape[0] // TILE):

        @pl.when(missing[i] > 0)
        def _(i=i):
            tiles[i * TILE : (i + 1) * TILE, :] = jnp.zeros((TILE, width), BF)

    for slot in range(len(places)):

        @pl.when(targets[slot] >= 0)
        def _(slot=slot):
            copy(slot).wait()

    kept = []
    for n in range(tiles.shape[0] // width):
        part = pl.ds(n * width, width)
        kept.append(pltpu.make_async_copy(tiles.at[part], near_out[n], out_sems.at[n]))
        kept[-1].start()
    for n in range(tiles.shape[0] // width):
        part = slice(n * width, (n + 1) * width)
        message_out[:, part] = mm_nt(solved[...], tiles[part, :]).astype(BF)
    for copy_out in kept:
        copy_out.wait()


def in_hbm(x):
    return pltpu.with_memory_space_constraint(x, pltpu.HBM)


def build(pieces, places, targets, missing, solved):
    width = solved.shape[1]
    near_rows = missing.shape[0] * TILE
    anywhere = pl.BlockSpec(memory_space=pl.ANY)
    held = pl.BlockSpec(memory_space=pltpu.HBM)
    return pl.pallas_call(
        functools.partial(build_kernel, places, len(pieces)),
        grid_spec=pltpu.PrefetchScalarGridSpec(
            num_scalar_prefetch=2,
            grid=(1,),
            in_specs=[held] * len(pieces) + [whole(solved)],
            out_specs=[anywhere] * (near_rows // width)
            + [pl.BlockSpec((ROWS, near_rows), lambda i, *_: (0, 0))],
            scratch_shapes=[
                pltpu.VMEM((near_rows, width), BF),
                pltpu.SemaphoreType.DMA((len(places),)),
                pltpu.SemaphoreType.DMA((near_rows // width,)),
            ],
        ),
        out_shape=[jax.ShapeDtypeStruct((width, width), BF)]
        + [pltpu.HBM((width, width), BF)] * (near_rows // width - 1)
        + [jax.ShapeDtypeStruct((ROWS, near_rows), BF)],
        compiler_params=pltpu.CompilerParams(vmem_limit_bytes=VMEM_LIMIT),
        cost_estimate=pl.CostEstimate(
            flops=300 * width * width, bytes_accessed=15 * width * width, transcendentals=0
        ),
    )(targets, missing, *map(in_hbm, pieces), solved)


def loads(sources, targets):
    groups = []
    sems = targets.pop() if sources else None
    for n, (source, target) in enumerate(zip(sources, targets)):
        rows = source.shape[0] // PARTS
        groups.append([])
        for i in range(PARTS):
            part = pl.ds(i * rows, rows)
            copy = pltpu.make_async_copy(source.at[part], target.at[part], sems.at[n * PARTS + i])
            copy.start()
            groups[-1].append(copy)

    def wait():
        for copy in groups.pop(0):
            copy.wait()

    return wait


def forward_kernel(panels, resident, *rest):
    near, held = rest[:panels], rest[panels : panels + resident]
    acc, received, inverse, coupling, *rest = rest[panels + resident :]
    acc_out, solved_out, message_out, *tiles = rest
    wait = loads(near, tiles)
    tiles = [*held, *tiles]
    width = acc.shape[1]
    residue = acc[...] - received[:, :width].astype(F32)
    acc_out[...] = residue
    store_halves(solved_out, *lower_solve(residue, inverse, coupling))
    for n in range(resident + panels):
        if n >= resident:
            wait()
        product = mm_nt(solved_out[...], tiles[n][...])
        passed = received[:, (n + 1) * width : (n + 2) * width].astype(F32)
        message_out[:, n * width : (n + 1) * width] = (product + passed).astype(BF)


def turn_kernel(acc, received, owed, inverse, coupling, solved_out, residue_out, message_out):
    residue = acc[...] - received[...].astype(F32)
    store_halves(solved_out, *lower_solve(residue, inverse, coupling))
    residue = solved_out[...].astype(F32) - owed[...]
    residue_out[...] = residue
    store_halves(message_out, *upper_solve(residue, inverse, coupling))


def backward_kernel(panels, resident, *rest):
    near, held = rest[:panels], rest[panels : panels + resident]
    acc, received, inverse, coupling, *rest = rest[panels + resident :]
    acc_out, message_out, *tiles = rest
    wait = loads(near, tiles)
    tiles = [*held, *tiles]
    width = acc.shape[1]
    if message_out.shape[1] > width:
        message_out[:, width:] = received[...]
    residue = acc[...]
    for n in range(resident + panels):
        if n >= resident:
            wait()
        residue = residue - mm(received[:, n * width : (n + 1) * width], tiles[n][...])
    acc_out[...] = residue
    store_halves(message_out, *upper_solve(residue, inverse, coupling))


def whole(x):
    return pl.BlockSpec(x.shape, lambda i, *_: (0,) * len(x.shape))


def step_call(kernel, near, operands, out_shapes, resident=0):
    width = out_shapes[0].shape[1]
    count = len(near)
    return pl.pallas_call(
        functools.partial(kernel, count, resident) if resident else kernel,
        grid=(1,),
        in_specs=[pl.BlockSpec(memory_space=pltpu.HBM)] * count + [whole(x) for x in operands],
        out_specs=[whole(x) for x in out_shapes],
        out_shape=out_shapes,
        scratch_shapes=[pltpu.VMEM(x.shape, x.dtype) for x in near]
        + ([pltpu.SemaphoreType.DMA((count * PARTS,))] if near else []),
        compiler_params=pltpu.CompilerParams(vmem_limit_bytes=VMEM_LIMIT),
        cost_estimate=pl.CostEstimate(
            flops=100 * width * width, bytes_accessed=5 * width * width, transcendentals=0
        ),
    )(*map(in_hbm, near), *operands)


def streamed(heights, pieces, held, sems):
    copies, at = [], 0
    for n, height in enumerate(heights):
        target = held.at[pl.ds(at, height)]
        copies.append(pltpu.make_async_copy(pieces[n], target, sems.at[n]))
        copies[n].start()
        at += height
    first = at = 0
    for n, height in enumerate(heights):
        copies[n].wait()
        at += height
        if at - first >= GROUP_ROWS or n == len(heights) - 1:
            yield slice(first, at)
            first = at


def collect_kernel(heights, rows, *rest, started):
    count = len(heights)
    out, held, sems = rest[count + started :]
    total = rest[count][...] if started else None
    for here in streamed(heights, rest[:count], held, sems):
        product = mm(rows[:, here], held[here, :])
        total = product if total is None else total + product
    out[...] = total


def spread_kernel(heights, solved, *rest):
    count = len(heights)
    out, held, sems = rest[count:]
    for here in streamed(heights, rest[:count], held, sems):
        out[:, here] = mm_nt(solved[...], held[here, :])


def arrange_kernel(order, rows, out):
    lanes = 2 * TILE
    right = lax.broadcasted_iota(jnp.int32, (ROWS, lanes), 1) >= TILE
    tiles = rows.shape[1] // TILE

    def half(n, want):
        tile = order[n]
        held_at = jnp.minimum(tile, tiles - 1)
        start = pl.multiple_of(lax.shift_right_logical(held_at, 1) * lanes, lanes)
        pair = rows[:, pl.ds(start, lanes)]
        turned = jnp.where((held_at & 1) == want, pair, pltpu.roll(pair, TILE, 1))
        return jnp.where(tile < tiles, turned, 0.0)

    for n in range(0, out.shape[1] // TILE, 2):
        both = jnp.where(right, half(n + 1, 1), half(n, 0))
        out[:, n * TILE : (n + 2) * TILE] = both.astype(BF)


def arrange(order, rows):
    out_shape = jax.ShapeDtypeStruct((ROWS, order.shape[0] * TILE), BF)
    return pl.pallas_call(
        arrange_kernel,
        grid_spec=pltpu.PrefetchScalarGridSpec(
            num_scalar_prefetch=1,
            grid=(1,),
            in_specs=[whole(rows)],
            out_specs=whole(out_shape),
        ),
        out_shape=out_shape,
        compiler_params=pltpu.CompilerParams(vmem_limit_bytes=VMEM_LIMIT),
        cost_estimate=pl.CostEstimate(
            flops=50_000_000, bytes_accessed=4_000_000, transcendentals=0
        ),
    )(order, rows)


def stream(kernel, pieces, operands, out_shape, started=()):
    width = pieces[0].shape[1]
    heights = [p.shape[0] for p in pieces]
    total = sum(heights)
    inputs = [*operands, *map(in_hbm, pieces), *started]
    specs = [whole(x) for x in operands]
    specs += [pl.BlockSpec(memory_space=pltpu.HBM)] * len(pieces) + [whole(x) for x in started]
    return pl.pallas_call(
        functools.partial(kernel, heights),
        grid=(1,),
        in_specs=specs,
        out_specs=whole(out_shape),
        scratch_shapes=[
            pltpu.VMEM((total, width), BF),
            pltpu.SemaphoreType.DMA((len(pieces),)),
        ],
        out_shape=out_shape,
        compiler_params=pltpu.CompilerParams(vmem_limit_bytes=VMEM_LIMIT),
        cost_estimate=pl.CostEstimate(
            flops=32 * width * total, bytes_accessed=2 * width * total, transcendentals=0
        ),
    )(*inputs)


def after(x, *others):
    return lax.optimization_barrier((x, *others))[0]


class Block:
    def __init__(self, array, tags):
        self.array, self.tags = array, tags

    def head(self, tiles):
        return Block(None if self.array is None else self.array[: tiles * TILE], self.tags[:tiles])

    def tail(self, tiles):
        return Block(None if self.array is None else self.array[tiles * TILE :], self.tags[tiles:])

    def after(self, *others):
        others = [o.array if isinstance(o, Block) else o for o in others]
        return Block(None if self.array is None else after(self.array, *others), self.tags)


def joined(*blocks):
    arrays = [b.array for b in blocks]
    array = None if arrays[0] is None else jnp.concatenate(arrays, axis=0)
    return Block(array, [t for b in blocks for t in b.tags])


def blk_index(z, x, c):
    return ((z % SIZE_Z) * SIZE_X + x % SIZE_X) * CORES + c


def blk_permute(array, target):
    pairs = [
        (blk_index(z, x, c), blk_index(*target(z, x, c)))
        for z in range(SIZE_Z)
        for x in range(SIZE_X)
        for c in range(CORES)
    ]
    return None if array is None else lax.ppermute(array, "blk", pairs)


def ring_z(block):
    array = blk_permute(block.array, lambda z, x, c: (z + 1 - 2 * c, x, c))
    return Block(array, [(dz + 1, dx, f, t) for dz, dx, f, t in block.tags])


def ring_x(block):
    array = blk_permute(block.array, lambda z, x, c: (z, x + 1 - 2 * c, c))
    return Block(array, [(dz, dx + 1, f, t) for dz, dx, f, t in block.tags])


def swap(block):
    array = blk_permute(block.array, lambda z, x, c: (z, x, 1 - c))
    return Block(array, [(-dz, -dx, 1 - f, t) for dz, dx, f, t in block.tags])


def gather_plane(own, beside):
    own = Block(own, [(0, 0, 0, 0), (0, 0, 0, 1)])
    other = swap(own)
    b = joined(own.tail(1), other.tail(1))
    a = joined(own.head(1), other.head(1))
    b_x = ring_x(b)
    a_1 = ring_z(a)
    n_1 = ring_z(b)
    b_far = ring_x(b_x.head(1))
    a_2 = ring_z(a_1)
    n_2 = ring_z(n_1)
    left = joined(b_x, b_far)
    l1 = ring_z(left)
    right = swap(left)
    a_3 = ring_z(a_2)
    early = joined(own.head(1), a_1, a_2)
    early_x = ring_x(early)
    m1 = ring_z(right)
    early_s = swap(early)
    n_3 = ring_z(n_2)
    early_sx = ring_x(early_s)
    l2 = ring_z(l1.after(early_s))
    s_l1 = swap(l1)
    a_4 = ring_z(a_3.head(1))
    early_far = ring_x(early_x.after(s_l1))
    s_early_x = swap(early_x)
    m2 = ring_z(m1)
    s_m1 = swap(m1)
    n_4 = ring_z(n_3.head(1).after(s_early_x))
    s_early_sx = swap(early_sx.after(n_3, s_m1))
    l3 = ring_z(l2.after(early_sx))
    s_l2 = swap(l2)
    late = joined(a_3, a_4)
    late_x = ring_x(late.after(s_early_sx, *beside))
    late_s = swap(late)
    late_sx = ring_x(late_s.after(s_l2))
    s_early_far = swap(early_far.after(late_s))
    m3 = ring_z(m2)
    s_m2 = swap(m2)
    n_all = joined(n_1, n_2, n_3, n_4)
    s_n = swap(n_all)
    late_far = ring_x(late_x.after(s_early_far, s_m2))
    s_late_x = swap(late_x)
    l4 = ring_z(l3.after(s_n))
    s_l3 = swap(l3)
    s_late_sx = swap(late_sx.after(s_late_x))
    s_m3 = swap(m3.after(s_l3))
    s_late_far = swap(late_far.after(s_late_sx, s_m3))
    s_l4 = swap(l4)
    blocks = [early, early_s, late, late_s, left, right, b, n_all, early_x, l1, m1, early_sx, l2, m2,
        early_far, late_x, l3, m3, late_sx, late_far, l4, s_n, s_early_x, s_l1, s_m1, s_early_sx, s_l2, s_m2,
        s_early_far, s_late_x, s_l3, s_m3, s_late_sx, s_late_far, s_l4]
    return blocks


def body(rhs, lower_factor_tiles, tile_rows, diag_inv, inner_block, lower_row_solution):
    _, cases, width = rhs.shape
    group = lax.axis_index("grp")
    inverse, coupling = diag_inv[0], inner_block[0]
    per_panel = width // TILE
    chain_tiles = GROUPS * per_panel
    lower_tiles = lower_row_solution.shape[1] // TILE
    tile_count = chain_tiles + lower_tiles
    rows_shape = lambda dtype, panels=1: jax.ShapeDtypeStruct((ROWS, panels * width), dtype)

    def grow(x):
        return jnp.pad(x, ((0, ROWS - cases), (0, 0)))

    def hop(x, source, target):
        return lax.ppermute(x, "grp", [(source, target)])

    def gathered(own, *beside):
        blocks = sorted(gather_plane(own, beside), key=lambda b: len(b.tags))
        return blocks[0::2] + blocks[1::2]

    blocks = gathered(None)
    places = [(n, i * TILE) for n, b in enumerate(blocks) for i in range(len(b.tags))]
    tags = [tag for b in blocks for tag in b.tags]
    slot_count = len(tags)
    split = len(blocks) // 2
    split_rows = sum(len(b.tags) for b in blocks[:split]) * TILE
    place_index = lax.axis_index("blk")
    core = place_index % CORES
    sign = 2 * core - 1
    dz, dx, flip, tile = (jnp.asarray(column, jnp.int32) for column in zip(*tags))
    source_z = (place_index // (SIZE_X * CORES) + sign * dz) % SIZE_Z
    source_x = (place_index // CORES + sign * dx) % SIZE_X
    source = (source_z * SIZE_X + source_x) * CORES + (core + flip) % CORES
    per_device = lower_factor_tiles.shape[1] // TILE
    slot_rows = tile_rows[0, 0][source * per_device + tile]

    first = (group + 1) * per_panel
    near_tiles = (GROUPS - 1) * per_panel
    targets = jnp.where(slot_rows < chain_tiles, slot_rows - first, -1)
    numbers = jnp.arange(near_tiles, dtype=jnp.int32)
    missing = jnp.all(targets[None, :] != numbers[:, None], axis=1).astype(jnp.int32)
    low_numbers = jnp.arange(chain_tiles, tile_count, dtype=jnp.int32)
    low_numbers = jnp.roll(low_numbers.reshape(GROUPS, -1), -group, axis=0).reshape(-1)
    here = slot_rows[None, :] == low_numbers[:, None]
    slot_numbers = jnp.arange(slot_count, dtype=jnp.int32)
    turned = jnp.min(jnp.where(here, slot_numbers[None, :], slot_count), axis=1)
    low_index = jnp.where(
        (slot_rows >= chain_tiles) & (slot_rows < tile_count), slot_rows - chain_tiles, lower_tiles
    )
    low_rows = grow(lower_row_solution).reshape(ROWS, lower_tiles, TILE)
    low_rows = jnp.pad(low_rows, ((0, 0), (0, 1), (0, 0)))[:, low_index, :]
    low_rows = low_rows.reshape(ROWS, slot_count * TILE)

    acc = grow(rhs[0]).astype(F32)
    (solved,) = step_call(first_kernel, [], [acc, inverse, coupling], [rows_shape(BF)])
    pieces = [
        b.array for b in gathered(lower_factor_tiles[0], solved, low_rows, targets, missing, turned)
    ]
    *near, message = build(pieces, places, targets, missing, solved)

    received = hop(message, 0, 1)
    owed = stream(
        functools.partial(collect_kernel, started=0), pieces[:split], [low_rows[:, :split_rows]],
        rows_shape(F32),
    )
    for step in (1, 2):
        panels = GROUPS - 1 - step
        acc, solved, message = step_call(
            forward_kernel, [], [*near[:panels], after(acc, owed), received, inverse, coupling],
            [rows_shape(F32), rows_shape(BF), rows_shape(BF, panels)], panels,
        )
        received = hop(message, step, step + 1)
        if step == 1:
            owed = stream(
                functools.partial(collect_kernel, started=1), pieces[split:],
                [low_rows[:, split_rows:]], rows_shape(F32), started=[owed],
            )
    solved, acc, message = step_call(
        turn_kernel, [], [acc, received, owed, inverse, coupling],
        [rows_shape(BF), rows_shape(F32), rows_shape(BF)],
    )

    received = hop(message, 3, 2)
    beyond = [
        stream(
            spread_kernel, pieces[:split], [solved], jax.ShapeDtypeStruct((ROWS, split_rows), F32)
        )
    ]
    acc, message = step_call(
        backward_kernel, [], [near[0], after(acc, *beyond), received, inverse, coupling],
        [rows_shape(F32), rows_shape(BF, 2)], 1,
    )
    received = hop(message, 2, 1)
    beyond.append(
        stream(
            spread_kernel, pieces[split:], [after(solved, message)],
            jax.ShapeDtypeStruct((ROWS, slot_count * TILE - split_rows), F32),
        )
    )
    acc, message = step_call(
        backward_kernel, [], [*near[:2], after(acc, *beyond), received, inverse, coupling],
        [rows_shape(F32), rows_shape(BF, 3)], 2,
    )
    received = hop(message, 1, 0)
    beyond = arrange(turned, after(jnp.concatenate(beyond, axis=1), message))[:cases]
    beyond = after(beyond, received)
    part = lower_tiles * TILE // GROUPS
    parts = [beyond[:, :part]] + [
        lax.ppermute(
            beyond[:, shift * part : (shift + 1) * part],
            "grp",
            [(g, (g + shift) % GROUPS) for g in range(GROUPS)],
        )
        for shift in range(1, GROUPS)
    ]
    acc, settled = step_call(
        backward_kernel, [], [*near, acc, received, inverse, coupling],
        [rows_shape(F32), rows_shape(BF)], 3,
    )
    pending = sum(p.astype(F32) for p in parts)
    return (solved[None, :cases], pending, settled[None, :cases])


def solution(mesh):
    placed = (
        P(None, "blk", "grp"),
        P(None, ("grp", "blk"), None),
        P(None, "grp", None),
        P(None, "grp", None),
        P(None, "grp", None),
        P("blk", None),
    )
    return jax.shard_map(
        body,
        mesh=mesh,
        in_specs=placed,
        out_specs=(P(None, "blk", "grp"), P("blk", "grp"), P(None, "blk", "grp")),
        check_vma=False,
    )
```
